32 devices in a mesh: ex: 16 (over z, y, core), tok: 2 (over x).
Axes of the slice: x: 2, y: 2, z: 4, core: 2. Of those that a mesh axis runs over, the one named last changes fastest.
Arguments:
- activations: bfloat16 [1024, 32, 4096], P(('ex', 'tok')), may hold values from -6 to 6
- out_grads: bfloat16 [1024, 32, 2, 1024], P(('ex', 'tok')), may hold values from -6 to 6
- block_len: int32 [1024], P(('ex', 'tok')), may hold values from 1 to 32
- block_dest: int32 [1024, 1], P(('ex', 'tok')), may hold values from 0 to 15; in each aligned block of 32 rows (0 to 31, 32 to 63, ...) at most 2 rows name the same one
- block_slot: int32 [1024], P(('ex', 'tok')), may hold values from 0 to 3
- in_proj: bfloat16 [4096, 128], replicated, may hold values from -0.09375 to 0.09375
- out_proj: bfloat16 [2, 1024, 64], replicated, may hold values from -0.1875 to 0.1875
- query_grads: float32 [32, 8192], P('ex'), may hold values from -6 to 6
- precond: float32 [2, 2, 64, 64], replicated, may hold values from -2 to 2, as said below
Outputs:
- scores: float32 [32, 64], P('tok', 'ex')
The draws below stay inside these ranges and needn't reach their ends.
Inputs may be any that keep to these rules, and one draw needn't show every extreme that they name: `block_dest`: among the 32 blocks of one device no index of ex is named more than 2 times, a bound that some device reaches; every index of ex is named by some block of the whole array. `precond`: entries of order one or less.
All inputs are finite; a program needn't handle non-finite values.
Results may differ from the reference program's by a relative error of at most 0.0003.
Values sent between devices are 32-bit elements; how exact they have to be, the bound alone decides.
No kernel may reach another device: no remote copies, remote signals or barrier semaphores. Data moves between devices by JAX's collectives and lax.ppermute only.
A program may use at most 64 MiB of HBM per device.

```python
import math
import jax
import jax.numpy as jnp
import numpy as np
from jax import lax

D = 4096
KV = 1024
R = 64
BLK = 32
NB = 32
CAP = 2
EX_DEV = 4
BLOCKS = 1024
EXAMPLES = 64
QRY = 32
F = 8192
N_EX = 16
N_TOK = 2


def draw_precond(key, part):
    first_key, second_key = jax.random.split(jax.random.fold_in(key, 17))
    diagonal = jax.random.uniform(first_key, (2, 2, R), jnp.float32, 0.6, 1.6)
    noise = jax.random.normal(second_key, (2, 2, R, R), jnp.float32)
    symmetric = (noise + jnp.swapaxes(noise, 2, 3)) * (0.35 / math.sqrt(2.0 * R))
    symmetric = jnp.clip(symmetric, -0.5, 0.5)
    identity = jnp.eye(R, dtype=jnp.float32)
    return symmetric * (1.0 - identity) + identity * diagonal[:, :, :, None]


def plant(result, key, smallest, largest):
    spot = [jax.random.randint(jax.random.fold_in(key, axis), (), 0, length) for axis, length in enumerate(result.shape)]
    longest = result.shape.index(max(result.shape))
    neighbour = spot[:longest] + [(spot[longest] + 1) % result.shape[longest]] + spot[longest + 1:]
    return result.at[tuple(spot)].set(smallest).at[tuple(neighbour)].set(largest)


def shard_levels(own_key, extent, cuts, least, top_value):
    loudness, own = 1.0, jax.random.fold_in(own_key, 6)
    for dim, blocks in cuts:
        draws = jnp.exp(jax.random.uniform(jax.random.fold_in(own, dim), (blocks,), jnp.float32, least / len(cuts), top_value / len(cuts)))
        loudness = loudness * jnp.repeat(draws, extent[dim] // blocks).reshape([-1 if axis == dim else 1 for axis in range(len(extent))])
    return loudness


def deal_out(own_key, own, number, rows, number_of, top, most, slope):
    order = jax.random.permutation(own_key, number_of)
    crowded, usual = shares(number_of, rows * top, most, slope, True), shares(number_of, rows * top, most, slope, False)
    places = jnp.arange(number_of)

    def named(tallies, turn):
        used = int((tallies > 0).sum())
        fixed = max(1, used // 4)
        shifted = fixed + (places - fixed + turn * (used - fixed)) % max(1, number_of - fixed)
        return jnp.zeros((number_of,), jnp.int32).at[order[jnp.where(places < fixed, places, shifted)]].set(jnp.asarray(tallies, jnp.int32))

    tallies = jnp.where(number % 4 == 0, named(crowded, number // 4), named(usual, number - number // 4 - 1))
    mixed = jax.random.permutation(jax.random.fold_in(own, 3), number_of)
    source_of, taker = mixed[0:number_of // 2 * 2:2], mixed[1:number_of // 2 * 2:2]
    room = jnp.minimum(tallies[source_of] - 1, most - tallies[taker]) // 2
    room = jnp.where((source_of == order[0]) | (taker == order[0]) | (tallies[taker] == 0), 0, jnp.maximum(room, 0))
    shifted = jax.random.randint(jax.random.fold_in(own, 4), (number_of // 2,), 0, 1 << 20) % (room + 1)
    tallies = tallies.at[source_of].add(-shifted).at[taker].add(shifted)
    labels = jnp.searchsorted(jnp.cumsum(tallies), jnp.arange(rows * top), side="right").astype(jnp.int32)
    listing = labels.reshape(top, rows).T
    listing = listing[jax.random.permutation(jax.random.fold_in(own, 1), rows)]
    turn = jax.random.randint(jax.random.fold_in(own, 2), (rows, 1), 0, top)
    return jnp.take_along_axis(listing, (jnp.arange(top)[None, :] + turn) % top, axis=1)


def shares(number_of, total, limit, slope, full):
    weights = [(1 << 20) // math.isqrt(rank ** slope) + 1 for rank in range(1, number_of + 1)]
    largest = limit if full else min(limit, max(-(-total // number_of), total * weights[0] // sum(weights)))
    least = 1 if total - largest >= number_of - 1 else 0
    counts, rest = [largest] + [least] * (number_of - 1), total - largest - least * (number_of - 1)
    while rest > 0:
        movable = [i for i in range(1, number_of) if counts[i] < largest] or [i for i in range(1, number_of) if counts[i] < limit]
        pool, left = sum([weights[i] for i in movable]), rest
        for i in movable:
            more = min(limit - counts[i], max(1, left * weights[i] // pool), rest)
            counts[i] = counts[i] + more
            rest = rest - more
    return np.array(counts)


def normal_values(rng, extent, width, limit, cuts=(), kind=jnp.bfloat16):
    values = width * jax.random.normal(rng, extent, jnp.float32)
    if cuts:
        values = values * shard_levels(rng, extent, cuts, -0.22, 0.18)
    return jnp.clip(values, -limit, limit).astype(kind)


def setup_inputs(seed: int = 0) -> dict:
    keys = jax.random.split(jax.random.key(seed), 10)
    activations = normal_values(keys[0], (BLOCKS, BLK, D), 1.0, 6.0, ((0, 32),))
    out_grads = normal_values(keys[1], (BLOCKS, BLK, 2, KV), 1.0, 6.0, ((0, 32),))
    block_len = plant(jax.random.randint(keys[2], (BLOCKS,), 1, BLK + 1), jax.random.fold_in(keys[2], 1), 1, BLK).astype(jnp.int32)
    block_dest_keys = jax.random.split(jax.random.fold_in(keys[3], 1), BLOCKS // NB)
    block_dest_turns = jax.random.permutation(jax.random.fold_in(keys[3], 3), BLOCKS // NB)
    block_dest = jax.vmap(lambda own, number: deal_out(jax.random.fold_in(keys[3], 2), own, number, NB, N_EX, 1, CAP, 2))(block_dest_keys, block_dest_turns).reshape((BLOCKS, 1))
    block_slot = plant(jax.random.randint(keys[4], (BLOCKS,), 0, EX_DEV), jax.random.fold_in(keys[4], 1), 0, EX_DEV - 1).astype(jnp.int32)
    in_proj = normal_values(keys[5], (D, 2 * R), D ** -0.5, 0.09375)
    out_proj = normal_values(keys[6], (2, KV, R), KV ** -0.5, 0.1875)
    query_grads = normal_values(keys[7], (QRY, F), 1.0, 6.0, ((0, 16),), jnp.float32)
    precond = draw_precond(jax.random.fold_in(keys[9], 71), 0)
    return dict(activations=activations, out_grads=out_grads, block_len=block_len, block_dest=block_dest, block_slot=block_slot, in_proj=in_proj, out_proj=out_proj, query_grads=query_grads, precond=precond)


highest = lax.Precision.HIGHEST


def block_terms(acts, grads, lens, in_proj, out_proj):
    count_blocks = acts.shape[0]
    size_block = acts.shape[1]
    proj_in = jnp.dot(acts.reshape(count_blocks * size_block, -1), in_proj, preferred_element_type=jnp.float32)
    proj_in = proj_in.reshape(count_blocks, size_block, 2, -1)
    proj_out = jnp.einsum("btlk,lkr->btlr", grads.astype(jnp.float32), out_proj.astype(jnp.float32), precision=highest)
    position = lax.broadcasted_iota(jnp.int32, (count_blocks, size_block), 1)
    live = (position < lens[:, None]).astype(jnp.float32)
    proj_out = proj_out * live[:, :, None, None]
    terms = jnp.einsum("btlo,btli->bloi", proj_out, proj_in, precision=highest)
    return terms.reshape(count_blocks, -1)


def reference(activations, out_grads, block_len, block_dest, block_slot, in_proj, out_proj, query_grads, precond):
    groups = N_EX * N_TOK

    def step(total, inputs):
        acts, grads, lens, target, owner_slot = inputs
        terms = block_terms(acts, grads, lens, in_proj, out_proj)
        example = target[:, 0] * EX_DEV + owner_slot
        onehot = (example[:, None] == jnp.arange(EXAMPLES, dtype=jnp.int32)[None, :]).astype(jnp.float32)
        return total + jnp.dot(onehot.T, terms, precision=highest), None

    features, _ = lax.scan(step, jnp.zeros((EXAMPLES, F), jnp.float32), (
        activations.reshape(groups, NB, BLK, D),
        out_grads.reshape(groups, NB, BLK, 2, KV),
        block_len.reshape(groups, NB),
        block_dest.reshape(groups, NB, 1),
        block_slot.reshape(groups, NB)))
    queries = query_grads.reshape(QRY, 2, R, R)
    left = jnp.einsum("lab,qlbc->qlac", precond[:, 0], queries, precision=highest)
    conditioned = jnp.einsum("qlac,lcd->qlad", left, precond[:, 1], precision=highest).reshape(QRY, F)
    return jnp.dot(conditioned, features.T, precision=highest) * (1.0 / (R * BLK))
```

```python
import jax
import jax.numpy as jnp
from jax import lax
from jax.experimental import pallas as pl
from jax.experimental.pallas import tpu as pltpu
from jax.sharding import PartitionSpec as P

EX_DEV = 4
SUB = 4
HIGHEST = lax.Precision.HIGHEST
NT = (((1,), (1,)), ((), ()))
TN = (((0,), (0,)), ((), ()))


def split(x):
    high = x.astype(jnp.bfloat16)
    return high, (x - high.astype(jnp.float32)).astype(jnp.bfloat16)


def mm(a, b, dims=(((1,), (0,)), ((), ()))):
    return lax.dot_general(a, b, dims, preferred_element_type=jnp.float32)


def split_mm(a, b, dims=(((1,), (0,)), ((), ()))):
    (ah, al), (bh, bl) = split(a), split(b)
    return mm(ah, bh, dims) + mm(al, bh, dims) + mm(ah, bl, dims)


def iota(shape, axis):
    return lax.broadcasted_iota(jnp.int32, shape, axis)


def features_kernel(
    core_ref, act_ref, out_ref, w_ref, precond_ref, id_ref, mine_ref, theirs_ref, right_ref, left_ref
):
    step = pl.program_id(0)
    blocks, size = act_ref.shape[0], act_ref.shape[1]
    r = precond_ref.shape[-1]
    half = r // 2
    rows = SUB * size

    @pl.when(step == 0)
    def _():
        row, col = iota((r, r), 0), iota((r, r), 1)
        order = (col == 2 * (row % half) + row // half).astype(jnp.float32)
        eye = (col == row).astype(jnp.float32)
        for l in range(2):
            left_ref[l] = lax.dot_general(
                order, precond_ref[l, 0], NT, precision=HIGHEST, preferred_element_type=jnp.float32
            )
            turned = lax.dot_general(
                eye, precond_ref[l, 1], NT, precision=HIGHEST, preferred_element_type=jnp.float32
            )
            both = jnp.concatenate([turned, turned], axis=1)
            zero = jnp.zeros_like(both)
            right_ref[l * r : (l + 1) * r] = jnp.concatenate(
                [both, zero] if l == 0 else [zero, both], axis=1
            )
        mine_ref[half] = jnp.broadcast_to(id_ref[...], mine_ref.shape[1:])
        theirs_ref[half] = jnp.broadcast_to(id_ref[...], theirs_ref.shape[1:])

    acts = act_ref[...].reshape(blocks * size, act_ref.shape[2])
    proj_in = split_mm(mm(acts, w_ref[...]), right_ref[...])
    core = core_ref[0]
    low_lane = iota((half, 2 * r), 1) < r
    lane_block = iota((r, rows), 1) // size
    outs = [split_mm(left_ref[l], out_ref[l], NT) for l in range(2)]
    for s in range(blocks // SUB):
        feats = []
        for l in range(2):
            oh, ol = split(outs[l][:, s * rows : (s + 1) * rows])
            ih, il = split(proj_in[s * rows : (s + 1) * rows, l * 2 * r : (l + 1) * 2 * r])
            zero = jnp.zeros_like(oh)
            lh = jnp.concatenate([jnp.where(lane_block == j, oh, zero) for j in range(SUB)], axis=0)
            ll = jnp.concatenate([jnp.where(lane_block == j, ol, zero) for j in range(SUB)], axis=0)
            got = mm(lh, ih) + mm(ll, ih) + mm(lh, il)
            feats.append(
                [
                    jnp.where(
                        low_lane,
                        got[j * r : j * r + half],
                        got[j * r + half : (j + 1) * r],
                    )
                    for j in range(SUB)
                ]
            )
        for j in range(SUB):
            b = step * blocks + s * SUB + j
            mine_ref[:half, pl.ds(b, 1), :] = jnp.where(core == 0, feats[0][j], feats[1][j])[:, None]
            theirs_ref[:half, pl.ds(b, 1), :] = jnp.where(core == 0, feats[1][j], feats[0][j])[:, None]


def scores_kernel(ex_count, tok_count, q_ref, mine_ref, other_ref, out_ref):
    half = mine_ref.shape[0] - 1
    queries = q_ref.shape[0] // half
    each = queries // tok_count
    acc = None
    for m in range(0, half, 2):
        q = jnp.concatenate([q_ref[pl.ds(m + d, queries, stride=half), :] for d in (0, 1)], axis=1)
        f = jnp.concatenate(
            [jnp.concatenate([ref[m + d] for d in (0, 1)], axis=1) for ref in (mine_ref, other_ref)],
            axis=0,
        )
        part = split_mm(f, q, NT)
        acc = part if acc is None else acc + part
    ids = jnp.concatenate([mine_ref[half], other_ref[half]], axis=0)[:, :1].astype(jnp.int32)
    blocks = acc.shape[0]
    wide = tok_count * EX_DEV * each
    lane = iota((queries, wide), 1)
    spread = (
        iota((queries, wide), 0) == lane // (EX_DEV * each) * each + lane % each
    ).astype(jnp.float32)
    spread = lax.dot_general(
        acc, spread, (((1,), (0,)), ((), ())), precision=HIGHEST, preferred_element_type=jnp.float32
    )
    lane = iota((blocks, wide), 1)
    spread = jnp.where(lane // each % EX_DEV == ids % EX_DEV, spread, 0.0)
    owner = (iota((blocks, ex_count * tok_count), 1) // tok_count == ids // EX_DEV).astype(jnp.float32)
    full = lax.dot_general(
        owner, spread, TN, precision=HIGHEST, preferred_element_type=jnp.float32
    )
    width = EX_DEV * each
    tok = iota((ex_count * tok_count, width), 0) % tok_count
    result = full[:, :width]
    for t in range(1, tok_count):
        result = jnp.where(tok == t, full[:, t * width : (t + 1) * width], result)
    out_ref[...] = result


def total_kernel(scale, in_ref, out_ref):
    total = jnp.sum(in_ref[...], axis=0, keepdims=True) * scale
    each = out_ref.shape[1]
    for k in range(out_ref.shape[0]):
        out_ref[pl.ds(k, 1), :] = total[:, k * each : (k + 1) * each]


def on_device(
    activations,
    out_grads,
    block_len,
    block_dest,
    block_slot,
    in_proj,
    out_proj,
    query_grads,
    precond,
):
    nb, size, depth = activations.shape
    layers, _, r = out_proj.shape
    half = r // 2
    ex_count, tok_count = lax.axis_size("ex"), lax.axis_size("tok")
    own_queries = query_grads.shape[0]
    queries = own_queries * ex_count
    core = lax.axis_index("ex") % 2

    pieces = query_grads.reshape(own_queries, layers, half, 2 * r)
    pieces = jnp.swapaxes(pieces, 0, 1).reshape(layers, own_queries * half, 2 * r)
    pieces = jnp.broadcast_to(pieces[None], (ex_count // 2,) + pieces.shape)
    pieces = pieces.reshape(ex_count, own_queries * half, 2 * r)
    gathered = lax.all_to_all(pieces, "ex", split_axis=0, concat_axis=0, tiled=True)

    live = lax.broadcasted_iota(jnp.int32, (nb, size), 1) < block_len[:, None]
    proj_out = jnp.einsum("btlk,lkr->lbtr", out_grads, out_proj, preferred_element_type=jnp.float32)
    proj_out = jnp.where(live[None, :, :, None], proj_out, 0.0).reshape(layers, nb * size, r)
    ids = (block_dest * EX_DEV + block_slot[:, None]).astype(jnp.float32)

    step_blocks = 8
    shape = jax.ShapeDtypeStruct((half + 1, nb, 2 * r), jnp.float32)
    whole = pl.BlockSpec((half + 1, nb, 2 * r), lambda i: (0, 0, 0))
    mine, theirs = pl.pallas_call(
        features_kernel,
        grid=(nb // step_blocks,),
        in_specs=[
            pl.BlockSpec(memory_space=pltpu.SMEM),
            pl.BlockSpec((step_blocks, size, depth), lambda i: (i, 0, 0)),
            pl.BlockSpec((layers, step_blocks * size, r), lambda i: (0, i, 0)),
            pl.BlockSpec((depth, layers * r), lambda i: (0, 0)),
            pl.BlockSpec((layers, 2, r, r), lambda i: (0, 0, 0, 0)),
            pl.BlockSpec((nb, 1), lambda i: (0, 0)),
        ],
        out_specs=[whole, whole],
        out_shape=[shape, shape],
        scratch_shapes=[
            pltpu.VMEM((layers * r, layers * 2 * r), jnp.float32),
            pltpu.VMEM((layers, r, r), jnp.float32),
        ],
        compiler_params=pltpu.CompilerParams(vmem_limit_bytes=32 * 1024 * 1024),
        cost_estimate=pl.CostEstimate(
            flops=2 * nb * size * depth * layers * r * 2,
            bytes_accessed=nb * size * depth * 2 + depth * layers * r * 2,
            transcendentals=0,
        ),
        name="features",
    )(core[None], activations, proj_out, in_proj, precond, ids)

    other = lax.ppermute(theirs, "ex", [(i, i ^ 1) for i in range(ex_count)])

    width = EX_DEV * queries // tok_count
    chunks = pl.pallas_call(
        lambda *refs: scores_kernel(ex_count, tok_count, *refs),
        out_shape=jax.ShapeDtypeStruct((ex_count * tok_count, width), jnp.float32),
        name="scores",
    )(gathered.reshape(queries * half, 2 * r), mine, other)
    arrived = lax.all_to_all(chunks, ("ex", "tok"), split_axis=0, concat_axis=0, tiled=True)
    total = pl.pallas_call(
        lambda *refs: total_kernel(1.0 / (r * size), *refs),
        out_shape=jax.ShapeDtypeStruct((EX_DEV, queries // tok_count), jnp.float32),
        name="total",
    )(arrived)
    return total.T


def solution(mesh):
    placed = (
        P(("ex", "tok"), None, None),
        P(("ex", "tok"), None, None, None),
        P(("ex", "tok")),
        P(("ex", "tok"), None),
        P(("ex", "tok")),
        P(),
        P(),
        P("ex", None),
        P(),
    )
    return jax.shard_map(
        on_device, mesh=mesh, in_specs=placed, out_specs=P("tok", "ex"), check_vma=False
    )
```

```python
import jax
import jax.numpy as jnp
from jax import lax
from jax.experimental import pallas as pl
from jax.experimental.pallas import tpu as pltpu
from jax.sharding import PartitionSpec as P

EX_DEV = 4
SUB = 4
STEP = 8
WIDE = 16
HIGHEST = lax.Precision.HIGHEST
PLAIN = (((1,), (0,)), ((), ()))
NT = (((1,), (1,)), ((), ()))
TN = (((0,), (0,)), ((), ()))
VMEM = pl.BlockSpec(memory_space=pltpu.VMEM)
SMEM = pl.BlockSpec(memory_space=pltpu.SMEM)


def split(x):
    high = x.astype(jnp.bfloat16)
    return high, (x - high.astype(jnp.float32)).astype(jnp.bfloat16)


def mm(a, b, dims=PLAIN):
    return lax.dot_general(a, b, dims, preferred_element_type=jnp.float32)


def exact(a, b, dims=PLAIN):
    return lax.dot_general(a, b, dims, precision=HIGHEST, preferred_element_type=jnp.float32)


def iota(shape, axis):
    return lax.broadcasted_iota(jnp.int32, shape, axis)


def diagonal(parts):
    zero = jnp.zeros_like(parts[0])
    return jnp.concatenate(
        [
            jnp.concatenate([x if k == l else zero for k in range(len(parts))], axis=1)
            for l, x in enumerate(parts)
        ],
        axis=0,
    )


def factors_kernel(precond_ref, left_ref, right_ref):
    layers, r = precond_ref.shape[0], precond_ref.shape[-1]
    row, col = iota((r, r), 0), iota((r, r), 1)
    order = (col == 2 * (row % (r // 2)) + row // (r // 2)).astype(jnp.float32)
    eye = (col == row).astype(jnp.float32)
    left = diagonal([exact(order, precond_ref[l, 0], NT) for l in range(layers)])
    left_ref[...] = jnp.concatenate(split(left), axis=0)
    turned = [exact(eye, precond_ref[l, 1], NT) for l in range(layers)]
    high, low = split(diagonal([jnp.concatenate([x, x], axis=1) for x in turned]))
    right_ref[...] = jnp.concatenate([high, high, low], axis=0)


def outputs_kernel(len_ref, grad_ref, w_ref, left_ref, out_ref, raw_ref):
    nb, size, layers, depth = grad_ref.shape
    width = left_ref.shape[1]
    rows = STEP * size
    lane_layer = iota((rows, width), 1) // (width // layers)
    slot = iota((size, width), 0)

    def turn(i, carry):
        grads = grad_ref[pl.ds(i * STEP, STEP)].reshape(rows * layers, depth)
        raw_ref[...] = mm(grads, w_ref[...], NT)
        out = raw_ref[pl.ds(0, rows, stride=layers), :]
        for l in range(1, layers):
            out = jnp.where(lane_layer == l, raw_ref[pl.ds(l, rows, stride=layers), :], out)
        live = jnp.concatenate([slot < len_ref[i * STEP + j] for j in range(STEP)], axis=0)
        high, low = split(jnp.where(live, out, 0.0))
        both = mm(left_ref[...], high, NT)
        done = both[:width] + both[width:] + mm(left_ref[:width], low, NT)
        here = pl.ds(pl.multiple_of(i * rows, rows), rows)
        out_ref[0, :, here], out_ref[1, :, here] = split(done)
        return carry

    lax.fori_loop(0, nb // STEP, turn, 0)


def features_kernel(act_ref, out_ref, w_ref, right_ref, feat_ref, whole_ref, in_ref):
    nb, size, depth = act_ref.shape
    width = out_ref.shape[1]
    layers = right_ref.shape[1] // feat_ref.shape[2]
    r = width // layers
    half = r // 2
    rows = SUB * size
    low_lane = iota((half, 2 * r), 1) < r
    lane_block = iota((r, rows), 1) // size

    def finish(i):
        high, low = split(in_ref[i % 2])
        proj_in = mm(jnp.concatenate([high, low], axis=1), right_ref[: 2 * width])
        proj_in = proj_in + mm(high, right_ref[2 * width :])
        for s in range(WIDE // SUB):
            start = (i * WIDE + s * SUB) * size
            for l in range(layers):
                outs = [out_ref[k, l * r : (l + 1) * r, start : start + rows] for k in (0, 1)]
                ih, il = split(proj_in[s * rows : (s + 1) * rows, l * 2 * r : (l + 1) * 2 * r])
                lhs = jnp.concatenate(
                    [
                        jnp.concatenate(
                            [jnp.where(lane_block == j, o, jnp.zeros_like(o)) for o in outs], axis=1
                        )
                        for j in range(SUB)
                    ],
                    axis=0,
                )
                rhs = jnp.concatenate(
                    [
                        jnp.concatenate([ih, il], axis=1),
                        jnp.concatenate([ih, jnp.zeros_like(il)], axis=1),
                    ],
                    axis=0,
                )
                got = mm(lhs, rhs)
                got = got[:, : 2 * r] + got[:, 2 * r :]
                for j in range(SUB):
                    b = i * WIDE + s * SUB + j
                    whole_ref[pl.ds(l * half * nb + b, half, stride=nb), :] = jnp.where(
                        low_lane, got[j * r : j * r + half], got[j * r + half : (j + 1) * r]
                    )

    for i in range(nb // WIDE):
        acts = act_ref[pl.ds(i * WIDE, WIDE)].reshape(WIDE * size, depth)
        in_ref[i % 2] = mm(acts, w_ref[...])
        if i > 0:
            finish(i - 1)
    finish(nb // WIDE - 1)
    for g in range(layers * half):
        feat_ref[g, :nb], feat_ref[g, nb:] = split(whole_ref[g * nb : (g + 1) * nb, :])


def scores_kernel(ex_count, tok_count, own, masks, place_ref, id_ref, first_ref, second_ref, feat_ref, out_ref):
    groups, nb, lanes = feat_ref.shape
    nb = nb // 2
    count = own * len(masks)
    acc = jnp.zeros((2 * nb, 2 * count), jnp.float32)
    for g in range(0, groups, 2):
        here = slice(g * lanes, (g + 2) * lanes)
        parts = [split(ref[:, here]) for ref in (first_ref, second_ref)]
        q = jnp.concatenate([p[k] for k in (0, 1) for p in parts], axis=0)
        acc = acc + mm(jnp.concatenate([feat_ref[g], feat_ref[g + 1]], axis=1), q, NT)
    acc = acc[:nb] + acc[nb:]
    acc = acc[:, :count] + acc[:, count:]

    queries = own * ex_count
    piece = iota((count, queries), 0) // own
    mask = jnp.zeros((count, queries), jnp.int32)
    for k, m in enumerate(masks):
        mask = jnp.where(piece == k, m, mask)
    query = jnp.bitwise_xor(mask, place_ref[0]) * own + iota((count, queries), 0) % own
    order = (query == iota((count, queries), 1)).astype(jnp.bfloat16)
    high, low = split(acc)
    acc = mm(high, order) + mm(low, order)
    targets = ex_count * tok_count * EX_DEV
    lane = iota((nb, targets), 1)
    owner = lane // EX_DEV // tok_count * EX_DEV + lane % EX_DEV == id_ref[...]
    owner = owner.astype(jnp.float32).astype(jnp.bfloat16)
    high, low = split(acc)
    full = mm(owner, high, TN) + mm(owner, low, TN)
    each = queries // tok_count
    tok = iota((targets, each), 0) // EX_DEV % tok_count
    result = full[:, :each]
    for t in range(1, tok_count):
        result = jnp.where(tok == t, full[:, t * each : (t + 1) * each], result)
    out_ref[...] = result


def on_device(
    activations,
    out_grads,
    block_len,
    block_dest,
    block_slot,
    in_proj,
    out_proj,
    query_grads,
    precond,
):
    nb, size, depth = activations.shape
    layers, grad_depth, r = out_proj.shape
    half = r // 2
    ex_count, tok_count = lax.axis_size("ex"), lax.axis_size("tok")
    own = query_grads.shape[0]
    place = lax.axis_index("ex").astype(jnp.int32)

    def swapped(x, mask):
        return lax.ppermute(x, "ex", [(i, i ^ mask) for i in range(ex_count)])

    width = layers * r
    left, right = pl.pallas_call(
        factors_kernel,
        out_shape=[
            jax.ShapeDtypeStruct((2 * width, width), jnp.bfloat16),
            jax.ShapeDtypeStruct((3 * width, 2 * width), jnp.bfloat16),
        ],
        compiler_params=pltpu.CompilerParams(vmem_limit_bytes=4 * 1024 * 1024),
        cost_estimate=pl.CostEstimate(flops=10**10, bytes_accessed=2**20, transcendentals=0),
        name="factors",
    )(precond)
    outs = pl.pallas_call(
        outputs_kernel,
        in_specs=[SMEM, VMEM, pl.BlockSpec(), pl.BlockSpec()],
        out_shape=jax.ShapeDtypeStruct((2, width, nb * size), jnp.bfloat16),
        scratch_shapes=[pltpu.VMEM((STEP * size * layers, width), jnp.float32)],
        compiler_params=pltpu.CompilerParams(vmem_limit_bytes=8 * 1024 * 1024),
        cost_estimate=pl.CostEstimate(flops=10**10, bytes_accessed=2**20, transcendentals=0),
        name="outputs",
    )(block_len, out_grads, jnp.swapaxes(out_proj, 1, 2).reshape(width, grad_depth), left)

    held = [(0, query_grads)]
    bit = ex_count // 2
    while bit > 4:
        held = held + [(mask ^ bit, swapped(x, bit)) for mask, x in held]
        bit //= 2
    last = [bit] if bit == 2 else [4, 2, 6] if bit == 4 else []
    far = [(mask, lax.optimization_barrier((x, outs))[0]) for mask, x in held[1:]]
    held = held + [(m, swapped(query_grads, m)) for m in last]
    held = held + [(mask ^ m, swapped(x, m)) for mask, x in far for m in last]

    feats = pl.pallas_call(
        features_kernel,
        in_specs=[VMEM, pl.BlockSpec(), VMEM, pl.BlockSpec()],
        out_shape=jax.ShapeDtypeStruct((layers * half, 2 * nb, 2 * r), jnp.bfloat16),
        scratch_shapes=[
            pltpu.VMEM((layers * half * nb, 2 * r), jnp.float32),
            pltpu.VMEM((2, WIDE * size, width), jnp.float32),
        ],
        compiler_params=pltpu.CompilerParams(vmem_limit_bytes=12 * 1024 * 1024),
        cost_estimate=pl.CostEstimate(flops=10**10, bytes_accessed=2**20, transcendentals=0),
        name="features",
    )(activations, outs, in_proj, right)

    masks = [mask for mask, _ in held]
    first = jnp.concatenate([x for _, x in held], axis=0)
    first, feats = lax.optimization_barrier((first, feats))
    second = swapped(first, 1)
    masks = tuple(masks + [mask ^ 1 for mask in masks])

    each = own * ex_count // tok_count
    chunks = pl.pallas_call(
        lambda *refs: scores_kernel(ex_count, tok_count, own, masks, *refs),
        in_specs=[SMEM] + [pl.BlockSpec()] * 4,
        out_shape=jax.ShapeDtypeStruct((ex_count * tok_count * EX_DEV, each), jnp.float32),
        compiler_params=pltpu.CompilerParams(vmem_limit_bytes=12 * 1024 * 1024),
        name="scores",
    )(place[None], block_dest * EX_DEV + block_slot[:, None], first, second, feats)
    chunks = chunks.reshape(ex_count * tok_count, EX_DEV, each)
    arrived = lax.all_to_all(chunks, ("ex", "tok"), split_axis=0, concat_axis=0, tiled=True)
    return jnp.sum(arrived, axis=0).T * (1.0 / (r * size))


def solution(mesh):
    placed = (
        P(("ex", "tok"), None, None),
        P(("ex", "tok"), None, None, None),
        P(("ex", "tok")),
        P(("ex", "tok"), None),
        P(("ex", "tok")),
        P(),
        P(),
        P("ex", None),
        P(),
    )
    return jax.shard_map(
        on_device, mesh=mesh, in_specs=placed, out_specs=P("tok", "ex"), check_vma=False
    )
```

```python
import jax
import jax.numpy as jnp
from jax import lax
from jax.experimental import pallas as pl
from jax.experimental.pallas import tpu as pltpu
from jax.sharding import PartitionSpec as P

EX_DEV = 4
SUB = 4
STEP = 8
WIDE = 16
HIGHEST = lax.Precision.HIGHEST
PLAIN = (((1,), (0,)), ((), ()))
NT = (((1,), (1,)), ((), ()))
TN = (((0,), (0,)), ((), ()))
VMEM = pl.BlockSpec(memory_space=pltpu.VMEM)
SMEM = pl.BlockSpec(memory_space=pltpu.SMEM)


def split(x):
    high = x.astype(jnp.bfloat16)
    return high, (x - high.astype(jnp.float32)).astype(jnp.bfloat16)


def mm(a, b, dims=PLAIN):
    return lax.dot_general(a, b, dims, preferred_element_type=jnp.float32)


def exact(a, b, dims=PLAIN):
    return lax.dot_general(a, b, dims, precision=HIGHEST, preferred_element_type=jnp.float32)


def iota(shape, axis):
    return lax.broadcasted_iota(jnp.int32, shape, axis)


def diagonal(parts):
    zero = jnp.zeros_like(parts[0])
    return jnp.concatenate(
        [
            jnp.concatenate([x if k == l else zero for k in range(len(parts))], axis=1)
            for l, x in enumerate(parts)
        ],
        axis=0,
    )


def factors_kernel(precond_ref, left_ref, right_ref):
    layers, r = precond_ref.shape[0], precond_ref.shape[-1]
    row, col = iota((r, r), 0), iota((r, r), 1)
    order = (col == 2 * (row % (r // 2)) + row // (r // 2)).astype(jnp.float32)
    eye = (col == row).astype(jnp.float32)
    left = diagonal([exact(order, precond_ref[l, 0], NT) for l in range(layers)])
    left_ref[...] = jnp.concatenate(split(left), axis=0)
    turned = [exact(eye, precond_ref[l, 1], NT) for l in range(layers)]
    high, low = split(diagonal([jnp.concatenate([x, x], axis=1) for x in turned]))
    right_ref[...] = jnp.concatenate([high, high, low], axis=0)


def outputs_kernel(len_ref, grad_ref, w_ref, left_ref, out_ref, raw_ref):
    nb, size, layers, depth = grad_ref.shape
    width = left_ref.shape[1]
    rows = STEP * size
    lane_layer = iota((rows, width), 1) // (width // layers)
    slot = iota((size, width), 0)

    def turn(i, carry):
        grads = grad_ref[pl.ds(i * STEP, STEP)].reshape(rows * layers, depth)
        raw_ref[...] = mm(grads, w_ref[...], NT)
        out = raw_ref[pl.ds(0, rows, stride=layers), :]
        for l in range(1, layers):
            out = jnp.where(lane_layer == l, raw_ref[pl.ds(l, rows, stride=layers), :], out)
        live = jnp.concatenate([slot < len_ref[i * STEP + j] for j in range(STEP)], axis=0)
        high, low = split(jnp.where(live, out, 0.0))
        both = mm(left_ref[...], high, NT)
        done = both[:width] + both[width:] + mm(left_ref[:width], low, NT)
        here = pl.ds(pl.multiple_of(i * rows, rows), rows)
        out_ref[0, :, here], out_ref[1, :, here] = split(done)
        return carry

    lax.fori_loop(0, nb // STEP, turn, 0)


def features_kernel(dest_ref, slot_ref, act_ref, out_ref, w_ref, right_ref, feat_ref, in_ref):
    nb, size, depth = act_ref.shape
    width = out_ref.shape[1]
    layers = right_ref.shape[1] // feat_ref.shape[1]
    r = width // layers
    half = r // 2
    rows = SUB * size
    low_lane = iota((half, 2 * r), 1) < r
    lane_block = iota((r, rows), 1) // size

    def finish(i):
        high, low = split(in_ref[i % 2])
        proj_in = mm(jnp.concatenate([high, low], axis=1), right_ref[: 2 * width])
        proj_in = proj_in + mm(high, right_ref[2 * width :])
        for s in range(WIDE // SUB):
            start = (i * WIDE + s * SUB) * size
            for l in range(layers):
                outs = [out_ref[k, l * r : (l + 1) * r, start : start + rows] for k in (0, 1)]
                ih, il = split(proj_in[s * rows : (s + 1) * rows, l * 2 * r : (l + 1) * 2 * r])
                lhs = jnp.concatenate(
                    [
                        jnp.concatenate(
                            [jnp.where(lane_block == j, o, jnp.zeros_like(o)) for o in outs], axis=1
                        )
                        for j in range(SUB)
                    ],
                    axis=0,
                )
                rhs = jnp.concatenate(
                    [
                        jnp.concatenate([ih, il], axis=1),
                        jnp.concatenate([ih, jnp.zeros_like(il)], axis=1),
                    ],
                    axis=0,
                )
                got = mm(lhs, rhs)
                got = got[:, : 2 * r] + got[:, 2 * r :]
                for j in range(SUB):
                    b = i * WIDE + s * SUB + j
                    feat_ref[pl.ds(l * half * nb + b, half, stride=nb), :] = jnp.where(
                        low_lane, got[j * r : j * r + half], got[j * r + half : (j + 1) * r]
                    )

    for i in range(nb // WIDE):
        acts = act_ref[pl.ds(i * WIDE, WIDE)].reshape(WIDE * size, depth)
        in_ref[i % 2] = mm(acts, w_ref[...])
        if i > 0:
            finish(i - 1)
    finish(nb // WIDE - 1)
    for b in range(nb):
        example = (dest_ref[b] * EX_DEV + slot_ref[b]).astype(jnp.float32)
        feat_ref[pl.ds(layers * half * nb + b, 1), :] = jnp.full((1, 2 * r), example)


def products(pieces, feat_ref):
    lanes = feat_ref.shape[1]
    groups = pieces[0].shape[1] // lanes
    nb = feat_ref.shape[0] // (groups + 1)
    count = sum(ref.shape[0] for ref in pieces)
    acc = jnp.zeros((2 * nb, 2 * count), jnp.float32)
    for g in range(0, groups, 2):
        q = jnp.concatenate([ref[:, g * lanes : (g + 2) * lanes] for ref in pieces], axis=0)
        f = [feat_ref[(g + d) * nb : (g + d + 1) * nb, :] for d in (0, 1)]
        f = jnp.concatenate(f, axis=1)
        q, f = [jnp.concatenate(split(x), axis=0) for x in (q, f)]
        acc = acc + mm(f, q, NT)
    acc = acc[:nb] + acc[nb:]
    return acc[:, :count] + acc[:, count:]


def own_scores_kernel(*refs):
    *pieces, mine_ref, out_ref = refs
    out_ref[...] = products(pieces, mine_ref)


def scores_kernel(ex_count, tok_count, own, masks, place_ref, *refs):
    *pieces, own_ref, dest_ref, other_ref, out_ref = refs
    acc = jnp.concatenate([own_ref[...], products(pieces, other_ref)], axis=0)
    blocks, count = acc.shape

    queries = own * ex_count
    piece = iota((count, queries), 0) // own
    mask = jnp.zeros((count, queries), jnp.int32)
    for k, m in enumerate(masks):
        mask = jnp.where(piece == k, m, mask)
    query = jnp.bitwise_xor(mask, place_ref[0]) * own + iota((count, queries), 0) % own
    order = (query == iota((count, queries), 1)).astype(jnp.float32).astype(jnp.bfloat16)
    high, low = split(acc)
    acc = mm(high, order) + mm(low, order)
    targets = ex_count * tok_count * EX_DEV
    lane = iota((blocks, targets), 1)
    ids = [ref[ref.shape[0] - blocks // 2 :, :1] for ref in (dest_ref, other_ref)]
    ids = jnp.concatenate(ids, axis=0).astype(jnp.int32)
    owner = lane // EX_DEV // tok_count * EX_DEV + lane % EX_DEV == ids
    owner = owner.astype(jnp.float32).astype(jnp.bfloat16)
    high, low = split(acc)
    full = mm(owner, high, TN) + mm(owner, low, TN)
    each = queries // tok_count
    tok = iota((targets, each), 0) // EX_DEV % tok_count
    result = full[:, :each]
    for t in range(1, tok_count):
        result = jnp.where(tok == t, full[:, t * each : (t + 1) * each], result)
    out_ref[...] = result


def on_device(
    activations,
    out_grads,
    block_len,
    block_dest,
    block_slot,
    in_proj,
    out_proj,
    query_grads,
    precond,
):
    nb, size, depth = activations.shape
    layers, grad_depth, r = out_proj.shape
    half = r // 2
    ex_count, tok_count = lax.axis_size("ex"), lax.axis_size("tok")
    own = query_grads.shape[0]
    place = lax.axis_index("ex").astype(jnp.int32)

    def swapped(x, mask):
        return lax.ppermute(x, "ex", [(i, i ^ mask) for i in range(ex_count)])

    width = layers * r
    left, right = pl.pallas_call(
        factors_kernel,
        out_shape=[
            jax.ShapeDtypeStruct((2 * width, width), jnp.bfloat16),
            jax.ShapeDtypeStruct((3 * width, 2 * width), jnp.bfloat16),
        ],
        compiler_params=pltpu.CompilerParams(vmem_limit_bytes=4 * 1024 * 1024),
        cost_estimate=pl.CostEstimate(flops=10**10, bytes_accessed=2**20, transcendentals=0),
        name="factors",
    )(precond)
    outs = pl.pallas_call(
        outputs_kernel,
        in_specs=[SMEM, VMEM, pl.BlockSpec(), pl.BlockSpec()],
        out_shape=jax.ShapeDtypeStruct((2, width, nb * size), jnp.bfloat16),
        scratch_shapes=[pltpu.VMEM((STEP * size * layers, width), jnp.float32)],
        compiler_params=pltpu.CompilerParams(vmem_limit_bytes=8 * 1024 * 1024),
        cost_estimate=pl.CostEstimate(flops=10**10, bytes_accessed=2**20, transcendentals=0),
        name="outputs",
    )(block_len, out_grads, jnp.swapaxes(out_proj, 1, 2).reshape(width, grad_depth), left)

    held, masks = query_grads, [0]
    bit = ex_count // 2
    while bit > 4:
        held = jnp.concatenate([held, swapped(held, bit)], axis=0)
        masks = masks + [mask ^ bit for mask in masks]
        bit //= 2
    last = [bit] if bit == 2 else [2, 4, 6] if bit == 4 else []
    held, outs = lax.optimization_barrier((held, outs))
    pieces = [held] + [swapped(held, m) for m in last]
    masks = tuple(mask ^ m for m in [0] + last for mask in masks)

    mine = pl.pallas_call(
        features_kernel,
        in_specs=[SMEM, SMEM, VMEM, pl.BlockSpec(), VMEM, pl.BlockSpec()],
        out_shape=jax.ShapeDtypeStruct(((layers * half + 1) * nb, 2 * r), jnp.float32),
        scratch_shapes=[pltpu.VMEM((2, WIDE * size, width), jnp.float32)],
        compiler_params=pltpu.CompilerParams(vmem_limit_bytes=12 * 1024 * 1024),
        cost_estimate=pl.CostEstimate(flops=10**10, bytes_accessed=2**20, transcendentals=0),
        name="features",
    )(block_dest[:, 0], block_slot, activations, outs, in_proj, right)

    other = swapped(mine, 1)

    each = own * ex_count // tok_count
    own_scores = pl.pallas_call(
        own_scores_kernel,
        out_shape=jax.ShapeDtypeStruct((nb, own * len(masks)), jnp.float32),
        compiler_params=pltpu.CompilerParams(vmem_limit_bytes=8 * 1024 * 1024),
        cost_estimate=pl.CostEstimate(flops=10**10, bytes_accessed=2**20, transcendentals=0),
        name="own_scores",
    )(*pieces, mine)
    chunks = pl.pallas_call(
        lambda *refs: scores_kernel(ex_count, tok_count, own, masks, *refs),
        in_specs=[SMEM] + [pl.BlockSpec()] * (len(pieces) + 3),
        out_shape=jax.ShapeDtypeStruct((ex_count * tok_count * EX_DEV, each), jnp.float32),
        compiler_params=pltpu.CompilerParams(vmem_limit_bytes=8 * 1024 * 1024),
        name="scores",
    )(place[None], *pieces, own_scores, mine[layers * half * nb :], other)
    chunks = chunks.reshape(ex_count * tok_count, EX_DEV, each)
    arrived = lax.all_to_all(chunks, ("ex", "tok"), split_axis=0, concat_axis=0, tiled=True)
    return jnp.sum(arrived, axis=0).T * (1.0 / (r * size))


def solution(mesh):
    placed = (
        P(("ex", "tok"), None, None),
        P(("ex", "tok"), None, None, None),
        P(("ex", "tok")),
        P(("ex", "tok"), None),
        P(("ex", "tok")),
        P(),
        P(),
        P("ex", None),
        P(),
    )
    return jax.shard_map(
        on_device, mesh=mesh, in_specs=placed, out_specs=P("tok", "ex"), check_vma=False
    )
```

```python
import jax
import jax.numpy as jnp
from jax import lax
from jax.experimental import pallas as pl
from jax.experimental.pallas import tpu as pltpu
from jax.sharding import PartitionSpec as P

EX_DEV = 4
SUB = 4
STEP = 8
WIDE = 16
HIGHEST = lax.Precision.HIGHEST
PLAIN = (((1,), (0,)), ((), ()))
NT = (((1,), (1,)), ((), ()))
TN = (((0,), (0,)), ((), ()))
VMEM = pl.BlockSpec(memory_space=pltpu.VMEM)
SMEM = pl.BlockSpec(memory_space=pltpu.SMEM)


def split(x):
    high = x.astype(jnp.bfloat16)
    return high, (x - high.astype(jnp.float32)).astype(jnp.bfloat16)


def mm(a, b, dims=PLAIN):
    return lax.dot_general(a, b, dims, preferred_element_type=jnp.float32)


def exact(a, b, dims=PLAIN):
    return lax.dot_general(a, b, dims, precision=HIGHEST, preferred_element_type=jnp.float32)


def iota(shape, axis):
    return lax.broadcasted_iota(jnp.int32, shape, axis)


def diagonal(parts):
    zero = jnp.zeros_like(parts[0])
    return jnp.concatenate(
        [
            jnp.concatenate([x if k == l else zero for k in range(len(parts))], axis=1)
            for l, x in enumerate(parts)
        ],
        axis=0,
    )


def factors_kernel(precond_ref, left_ref, right_ref):
    layers, r = precond_ref.shape[0], precond_ref.shape[-1]
    row, col = iota((r, r), 0), iota((r, r), 1)
    order = (col == 2 * (row % (r // 2)) + row // (r // 2)).astype(jnp.float32)
    eye = (col == row).astype(jnp.float32)
    left = diagonal([exact(order, precond_ref[l, 0], NT) for l in range(layers)])
    left_ref[...] = jnp.concatenate(split(left), axis=0)
    turned = [exact(eye, precond_ref[l, 1], NT) for l in range(layers)]
    high, low = split(diagonal([jnp.concatenate([x, x], axis=1) for x in turned]))
    right_ref[...] = jnp.concatenate([high, high, low], axis=0)


def outputs_kernel(len_ref, grad_ref, w_ref, left_ref, out_ref, raw_ref):
    nb, size, layers, depth = grad_ref.shape
    width = left_ref.shape[1]
    rows = STEP * size
    lane_layer = iota((rows, width), 1) // (width // layers)
    slot = iota((size, width), 0)

    def turn(i, carry):
        grads = grad_ref[pl.ds(i * STEP, STEP)].reshape(rows * layers, depth)
        raw_ref[...] = mm(grads, w_ref[...], NT)
        out = raw_ref[pl.ds(0, rows, stride=layers), :]
        for l in range(1, layers):
            out = jnp.where(lane_layer == l, raw_ref[pl.ds(l, rows, stride=layers), :], out)
        live = jnp.concatenate([slot < len_ref[i * STEP + j] for j in range(STEP)], axis=0)
        high, low = split(jnp.where(live, out, 0.0))
        both = mm(left_ref[...], high, NT)
        done = both[:width] + both[width:] + mm(left_ref[:width], low, NT)
        here = pl.ds(pl.multiple_of(i * rows, rows), rows)
        out_ref[0, :, here], out_ref[1, :, here] = split(done)
        return carry

    lax.fori_loop(0, nb // STEP, turn, 0)


def features_kernel(dest_ref, slot_ref, act_ref, out_ref, w_ref, right_ref, feat_ref, in_ref):
    nb, size, depth = act_ref.shape
    width = out_ref.shape[1]
    layers = right_ref.shape[1] // feat_ref.shape[1]
    r = width // layers
    half = r // 2
    rows = SUB * size
    low_lane = iota((half, 2 * r), 1) < r
    lane_block = iota((r, rows), 1) // size

    def finish(i):
        high, low = split(in_ref[i % 2])
        proj_in = mm(jnp.concatenate([high, low], axis=1), right_ref[: 2 * width])
        proj_in = proj_in + mm(high, right_ref[2 * width :])
        for s in range(WIDE // SUB):
            start = (i * WIDE + s * SUB) * size
            for l in range(layers):
                outs = [out_ref[k, l * r : (l + 1) * r, start : start + rows] for k in (0, 1)]
                ih, il = split(proj_in[s * rows : (s + 1) * rows, l * 2 * r : (l + 1) * 2 * r])
                lhs = jnp.concatenate(
                    [
                        jnp.concatenate(
                            [jnp.where(lane_block == j, o, jnp.zeros_like(o)) for o in outs], axis=1
                        )
                        for j in range(SUB)
                    ],
                    axis=0,
                )
                rhs = jnp.concatenate(
                    [
                        jnp.concatenate([ih, il], axis=1),
                        jnp.concatenate([ih, jnp.zeros_like(il)], axis=1),
                    ],
                    axis=0,
                )
                got = mm(lhs, rhs)
                got = got[:, : 2 * r] + got[:, 2 * r :]
                for j in range(SUB):
                    b = i * WIDE + s * SUB + j
                    here = (b * layers + l) * half
                    feat_ref[here : here + half] = jnp.where(
                        low_lane, got[j * r : j * r + half], got[j * r + half : (j + 1) * r]
                    )

    for i in range(nb // WIDE):
        acts = act_ref[pl.ds(i * WIDE, WIDE)].reshape(WIDE * size, depth)
        in_ref[i % 2] = mm(acts, w_ref[...])
        if i > 0:
            finish(i - 1)
    finish(nb // WIDE - 1)
    for b in range(nb):
        example = (dest_ref[b] * EX_DEV + slot_ref[b]).astype(jnp.float32)
        feat_ref[pl.ds(layers * half * nb + b, 1), :] = jnp.full((1, 2 * r), example)


def products(pieces, feat_ref):
    lanes = feat_ref.shape[1]
    groups = pieces[0].shape[1] // lanes
    nb = feat_ref.shape[0] // (groups + 1)
    count = sum(ref.shape[0] for ref in pieces)
    acc = jnp.zeros((2 * nb, 2 * count), jnp.float32)
    for g in range(0, groups, 2):
        q = jnp.concatenate([ref[:, g * lanes : (g + 2) * lanes] for ref in pieces], axis=0)
        f = [feat_ref[pl.ds(g + d, nb, stride=groups), :] for d in (0, 1)]
        f = jnp.concatenate(f, axis=1)
        q, f = [jnp.concatenate(split(x), axis=0) for x in (q, f)]
        acc = acc + mm(f, q, NT)
    acc = acc[:nb] + acc[nb:]
    return acc[:, :count] + acc[:, count:]


def own_scores_kernel(*refs):
    *pieces, mine_ref, out_ref = refs
    out_ref[...] = products(pieces, mine_ref)


def scores_kernel(ex_count, tok_count, own, masks, place_ref, *refs):
    *pieces, own_ref, dest_ref, other_ref, out_ref = refs
    acc = jnp.concatenate([own_ref[...], products(pieces, other_ref)], axis=0)
    blocks, count = acc.shape

    queries = own * ex_count
    piece = iota((count, queries), 0) // own
    mask = jnp.zeros((count, queries), jnp.int32)
    for k, m in enumerate(masks):
        mask = jnp.where(piece == k, m, mask)
    query = jnp.bitwise_xor(mask, place_ref[0]) * own + iota((count, queries), 0) % own
    order = (query == iota((count, queries), 1)).astype(jnp.float32).astype(jnp.bfloat16)
    high, low = split(acc)
    acc = mm(high, order) + mm(low, order)
    targets = ex_count * tok_count
    lane = iota((blocks, targets * EX_DEV), 1)
    ids = [ref[ref.shape[0] - blocks // 2 :, :1] for ref in (dest_ref, other_ref)]
    ids = jnp.concatenate(ids, axis=0).astype(jnp.int32)
    owner = lane % targets // tok_count * EX_DEV + lane // targets == ids
    owner = owner.astype(jnp.float32).astype(jnp.bfloat16)
    high, low = split(acc)
    full = mm(owner, high, TN) + mm(owner, low, TN)
    each = queries // tok_count
    tok = iota((targets * EX_DEV, each), 0) % tok_count
    result = full[:, :each]
    for t in range(1, tok_count):
        result = jnp.where(tok == t, full[:, t * each : (t + 1) * each], result)
    out_ref[...] = jnp.concatenate(
        [result[k * targets : (k + 1) * targets] for k in range(EX_DEV)], axis=1
    )


def on_device(
    activations,
    out_grads,
    block_len,
    block_dest,
    block_slot,
    in_proj,
    out_proj,
    query_grads,
    precond,
):
    nb, size, depth = activations.shape
    layers, grad_depth, r = out_proj.shape
    half = r // 2
    ex_count, tok_count = lax.axis_size("ex"), lax.axis_size("tok")
    own = query_grads.shape[0]
    place = lax.axis_index("ex").astype(jnp.int32)

    def swapped(x, mask):
        return lax.ppermute(x, "ex", [(i, i ^ mask) for i in range(ex_count)])

    width = layers * r
    left, right = pl.pallas_call(
        factors_kernel,
        out_shape=[
            jax.ShapeDtypeStruct((2 * width, width), jnp.bfloat16),
            jax.ShapeDtypeStruct((3 * width, 2 * width), jnp.bfloat16),
        ],
        compiler_params=pltpu.CompilerParams(vmem_limit_bytes=4 * 1024 * 1024),
        cost_estimate=pl.CostEstimate(flops=10**10, bytes_accessed=2**20, transcendentals=0),
        name="factors",
    )(precond)
    outs = pl.pallas_call(
        outputs_kernel,
        in_specs=[SMEM, VMEM, pl.BlockSpec(), pl.BlockSpec()],
        out_shape=jax.ShapeDtypeStruct((2, width, nb * size), jnp.bfloat16),
        scratch_shapes=[pltpu.VMEM((STEP * size * layers, width), jnp.float32)],
        compiler_params=pltpu.CompilerParams(vmem_limit_bytes=8 * 1024 * 1024),
        cost_estimate=pl.CostEstimate(flops=10**10, bytes_accessed=2**20, transcendentals=0),
        name="outputs",
    )(block_len, out_grads, jnp.swapaxes(out_proj, 1, 2).reshape(width, grad_depth), left)

    held, masks = query_grads, [0]
    bit = ex_count // 2
    while bit > 4:
        held = jnp.concatenate([held, swapped(held, bit)], axis=0)
        masks = masks + [mask ^ bit for mask in masks]
        bit //= 2
    last = [bit] if bit == 2 else [6, 2, 4] if bit == 4 else []
    held, outs = lax.optimization_barrier((held, outs))
    pieces = [held] + [swapped(held, m) for m in last]
    masks = tuple(mask ^ m for m in [0] + last for mask in masks)

    mine = pl.pallas_call(
        features_kernel,
        in_specs=[SMEM, SMEM, VMEM, pl.BlockSpec(), VMEM, pl.BlockSpec()],
        out_shape=jax.ShapeDtypeStruct(((layers * half + 1) * nb, 2 * r), jnp.float32),
        scratch_shapes=[pltpu.VMEM((2, WIDE * size, width), jnp.float32)],
        compiler_params=pltpu.CompilerParams(vmem_limit_bytes=12 * 1024 * 1024),
        cost_estimate=pl.CostEstimate(flops=10**10, bytes_accessed=2**20, transcendentals=0),
        name="features",
    )(block_dest[:, 0], block_slot, activations, outs, in_proj, right)

    other = swapped(mine, 1)

    each = own * ex_count // tok_count
    own_scores = pl.pallas_call(
        own_scores_kernel,
        out_shape=jax.ShapeDtypeStruct((nb, own * len(masks)), jnp.float32),
        compiler_params=pltpu.CompilerParams(vmem_limit_bytes=8 * 1024 * 1024),
        cost_estimate=pl.CostEstimate(flops=10**10, bytes_accessed=2**20, transcendentals=0),
        name="own_scores",
    )(*pieces, mine)
    chunks = pl.pallas_call(
        lambda *refs: scores_kernel(ex_count, tok_count, own, masks, *refs),
        in_specs=[SMEM] + [pl.BlockSpec()] * (len(pieces) + 3),
        out_shape=jax.ShapeDtypeStruct((ex_count * tok_count, EX_DEV * each), jnp.float32),
        compiler_params=pltpu.CompilerParams(vmem_limit_bytes=8 * 1024 * 1024),
        name="scores",
    )(place[None], *pieces, own_scores, mine[layers * half * nb :], other)
    arrived = lax.all_to_all(chunks, ("ex", "tok"), split_axis=0, concat_axis=0, tiled=True)
    total = jnp.sum(arrived, axis=0) * (1.0 / (r * size))
    return total.reshape(EX_DEV, each).T


def solution(mesh):
    placed = (
        P(("ex", "tok"), None, None),
        P(("ex", "tok"), None, None, None),
        P(("ex", "tok")),
        P(("ex", "tok"), None),
        P(("ex", "tok")),
        P(),
        P(),
        P("ex", None),
        P(),
    )
    return jax.shard_map(
        on_device, mesh=mesh, in_specs=placed, out_specs=P("tok", "ex"), check_vma=False
    )
```

```python
import jax
import jax.numpy as jnp
from jax import lax
from jax.experimental import pallas as pl
from jax.experimental.pallas import tpu as pltpu
from jax.sharding import PartitionSpec as P

EX_DEV = 4
SUB = 4
STEP = 8
WIDE = 16
HIGHEST = lax.Precision.HIGHEST
PLAIN = (((1,), (0,)), ((), ()))
NT = (((1,), (1,)), ((), ()))
TN = (((0,), (0,)), ((), ()))
VMEM = pl.BlockSpec(memory_space=pltpu.VMEM)


def split(x):
    high = x.astype(jnp.bfloat16)
    return high, (x - high.astype(jnp.float32)).astype(jnp.bfloat16)


def mm(a, b, dims=PLAIN):
    return lax.dot_general(a, b, dims, preferred_element_type=jnp.float32)


def exact(a, b, dims=PLAIN):
    return lax.dot_general(a, b, dims, precision=HIGHEST, preferred_element_type=jnp.float32)


def iota(shape, axis):
    return lax.broadcasted_iota(jnp.int32, shape, axis)


def diagonal(parts):
    zero = jnp.zeros_like(parts[0])
    return jnp.concatenate(
        [
            jnp.concatenate([x if k == l else zero for k in range(len(parts))], axis=1)
            for l, x in enumerate(parts)
        ],
        axis=0,
    )


def factors_kernel(precond_ref, left_ref, right_ref):
    layers, r = precond_ref.shape[0], precond_ref.shape[-1]
    row, col = iota((r, r), 0), iota((r, r), 1)
    order = (col == 2 * (row % (r // 2)) + row // (r // 2)).astype(jnp.float32)
    eye = (col == row).astype(jnp.float32)
    left = diagonal([exact(order, precond_ref[l, 0], NT) for l in range(layers)])
    left_ref[...] = jnp.concatenate(split(left), axis=0)
    turned = [exact(eye, precond_ref[l, 1], NT) for l in range(layers)]
    high, low = split(diagonal([jnp.concatenate([x, x], axis=1) for x in turned]))
    right_ref[...] = jnp.concatenate([high, high, low], axis=0)


def outputs_kernel(len_ref, grad_ref, w_ref, left_ref, out_ref, raw_ref):
    nb, size, layers, depth = grad_ref.shape
    width = left_ref.shape[1]
    rows = STEP * size
    lane_layer = iota((rows, width), 1) // (width // layers)
    slot = iota((size, width), 0)

    def turn(i, carry):
        grads = grad_ref[pl.ds(i * STEP, STEP)].reshape(rows * layers, depth)
        raw_ref[...] = mm(grads, w_ref[...], NT)
        out = raw_ref[pl.ds(0, rows, stride=layers), :]
        for l in range(1, layers):
            out = jnp.where(lane_layer == l, raw_ref[pl.ds(l, rows, stride=layers), :], out)
        lens = [len_ref[pl.ds(i * STEP + j, 1), :] for j in range(STEP)]
        live = jnp.concatenate([slot < x for x in lens], axis=0)
        high, low = split(jnp.where(live, out, 0.0))
        both = mm(left_ref[...], high, NT)
        done = both[:width] + both[width:] + mm(left_ref[:width], low, NT)
        here = pl.ds(pl.multiple_of(i * rows, rows), rows)
        out_ref[0, :, here], out_ref[1, :, here] = split(done)
        return carry

    lax.fori_loop(0, nb // STEP, turn, 0)


def features_kernel(id_ref, act_ref, out_ref, w_ref, right_ref, feat_ref, in_ref):
    nb, size, depth = act_ref.shape
    width = out_ref.shape[1]
    layers = right_ref.shape[1] // feat_ref.shape[1]
    r = width // layers
    half = r // 2
    rows = SUB * size
    low_lane = iota((half, 2 * r), 1) < r
    lane_block = iota((r, rows), 1) // size

    def finish(i):
        high, low = split(in_ref[i % 2])
        proj_in = mm(jnp.concatenate([high, low], axis=1), right_ref[: 2 * width])
        proj_in = proj_in + mm(high, right_ref[2 * width :])
        for s in range(WIDE // SUB):
            start = (i * WIDE + s * SUB) * size
            for l in range(layers):
                outs = [out_ref[k, l * r : (l + 1) * r, start : start + rows] for k in (0, 1)]
                ih, il = split(proj_in[s * rows : (s + 1) * rows, l * 2 * r : (l + 1) * 2 * r])
                lhs = jnp.concatenate(
                    [
                        jnp.concatenate(
                            [jnp.where(lane_block == j, o, jnp.zeros_like(o)) for o in outs], axis=1
                        )
                        for j in range(SUB)
                    ],
                    axis=0,
                )
                rhs = jnp.concatenate(
                    [
                        jnp.concatenate([ih, il], axis=1),
                        jnp.concatenate([ih, jnp.zeros_like(il)], axis=1),
                    ],
                    axis=0,
                )
                got = mm(lhs, rhs)
                got = got[:, : 2 * r] + got[:, 2 * r :]
                for j in range(SUB):
                    b = i * WIDE + s * SUB + j
                    here = (b * layers + l) * half
                    feat_ref[here : here + half] = jnp.where(
                        low_lane, got[j * r : j * r + half], got[j * r + half : (j + 1) * r]
                    )

    for i in range(nb // WIDE):
        acts = act_ref[pl.ds(i * WIDE, WIDE)].reshape(WIDE * size, depth)
        in_ref[i % 2] = mm(acts, w_ref[...])
        if i > 0:
            finish(i - 1)
    finish(nb // WIDE - 1)
    feat_ref[layers * half * nb :] = id_ref[...]


def products(pieces, feat_ref):
    lanes = feat_ref.shape[1]
    groups = pieces[0].shape[1] // lanes
    nb = feat_ref.shape[0] // (groups + 1)
    count = sum(ref.shape[0] for ref in pieces)
    acc = jnp.zeros((2 * nb, 2 * count), jnp.float32)
    for g in range(0, groups, 2):
        q = jnp.concatenate([ref[:, g * lanes : (g + 2) * lanes] for ref in pieces], axis=0)
        f = [feat_ref[pl.ds(g + d, nb, stride=groups), :] for d in (0, 1)]
        f = jnp.concatenate(f, axis=1)
        q, f = [jnp.concatenate(split(x), axis=0) for x in (q, f)]
        acc = acc + mm(f, q, NT)
    acc = acc[:nb] + acc[nb:]
    return acc[:, :count] + acc[:, count:]


def own_scores_kernel(*refs):
    *pieces, mine_ref, out_ref = refs
    out_ref[...] = products(pieces, mine_ref)


def scores_kernel(ex_count, tok_count, own, masks, place_ref, *refs):
    *pieces, own_ref, dest_ref, other_ref, out_ref = refs
    acc = jnp.concatenate([own_ref[...], products(pieces, other_ref)], axis=0)
    blocks, count = acc.shape

    queries = own * ex_count
    piece = iota((count, queries), 0) // own
    mask = jnp.zeros((count, queries), jnp.int32)
    for k, m in enumerate(masks):
        mask = jnp.where(piece == k, m, mask)
    query = jnp.bitwise_xor(mask, place_ref[:, :1]) * own + iota((count, queries), 0) % own
    order = (query == iota((count, queries), 1)).astype(jnp.float32).astype(jnp.bfloat16)
    high, low = split(acc)
    acc = mm(high, order) + mm(low, order)
    targets = ex_count * tok_count
    lane = iota((blocks, targets * EX_DEV), 1)
    ids = [ref[ref.shape[0] - blocks // 2 :, :1] for ref in (dest_ref, other_ref)]
    ids = jnp.concatenate(ids, axis=0).astype(jnp.int32)
    owner = lane % targets // tok_count * EX_DEV + lane // targets == ids
    owner = owner.astype(jnp.float32).astype(jnp.bfloat16)
    high, low = split(acc)
    full = mm(owner, high, TN) + mm(owner, low, TN)
    each = queries // tok_count
    tok = iota((targets * EX_DEV, each), 0) % tok_count
    result = full[:, :each]
    for t in range(1, tok_count):
        result = jnp.where(tok == t, full[:, t * each : (t + 1) * each], result)
    out_ref[...] = jnp.concatenate(
        [result[k * targets : (k + 1) * targets] for k in range(EX_DEV)], axis=1
    )


def on_device(
    activations,
    out_grads,
    block_len,
    block_dest,
    block_slot,
    in_proj,
    out_proj,
    query_grads,
    precond,
):
    nb, size, depth = activations.shape
    layers, grad_depth, r = out_proj.shape
    half = r // 2
    ex_count, tok_count = lax.axis_size("ex"), lax.axis_size("tok")
    own = query_grads.shape[0]
    place = lax.axis_index("ex").astype(jnp.int32)

    def swapped(x, mask):
        return lax.ppermute(x, "ex", [(i, i ^ mask) for i in range(ex_count)])

    width = layers * r
    left, right = pl.pallas_call(
        factors_kernel,
        out_shape=[
            jax.ShapeDtypeStruct((2 * width, width), jnp.bfloat16),
            jax.ShapeDtypeStruct((3 * width, 2 * width), jnp.bfloat16),
        ],
        compiler_params=pltpu.CompilerParams(vmem_limit_bytes=4 * 1024 * 1024),
        cost_estimate=pl.CostEstimate(flops=10**10, bytes_accessed=2**20, transcendentals=0),
        name="factors",
    )(precond)
    lens = jnp.broadcast_to(block_len[:, None], (nb, width))
    outs = pl.pallas_call(
        outputs_kernel,
        in_specs=[pl.BlockSpec(), VMEM, pl.BlockSpec(), pl.BlockSpec()],
        out_shape=jax.ShapeDtypeStruct((2, width, nb * size), jnp.bfloat16),
        scratch_shapes=[pltpu.VMEM((STEP * size * layers, width), jnp.float32)],
        compiler_params=pltpu.CompilerParams(vmem_limit_bytes=8 * 1024 * 1024),
        cost_estimate=pl.CostEstimate(flops=10**10, bytes_accessed=2**20, transcendentals=0),
        name="outputs",
    )(lens, out_grads, jnp.swapaxes(out_proj, 1, 2).reshape(width, grad_depth), left)

    held, masks = query_grads, [0]
    bit = ex_count // 2
    while bit > 4:
        held = jnp.concatenate([held, swapped(held, bit)], axis=0)
        masks = masks + [mask ^ bit for mask in masks]
        bit //= 2
    last = [bit] if bit == 2 else [6, 2, 4] if bit == 4 else []
    held, outs = lax.optimization_barrier((held, outs))
    pieces = [held] + [swapped(held, m) for m in last]
    masks = tuple(mask ^ m for m in [0] + last for mask in masks)

    ids = (block_dest * EX_DEV + block_slot[:, None]).astype(jnp.float32)
    ids = jnp.broadcast_to(ids, (nb, 2 * r))
    mine = pl.pallas_call(
        features_kernel,
        in_specs=[pl.BlockSpec(), VMEM, pl.BlockSpec(), VMEM, pl.BlockSpec()],
        out_shape=jax.ShapeDtypeStruct(((layers * half + 1) * nb, 2 * r), jnp.float32),
        scratch_shapes=[pltpu.VMEM((2, WIDE * size, width), jnp.float32)],
        compiler_params=pltpu.CompilerParams(vmem_limit_bytes=12 * 1024 * 1024),
        cost_estimate=pl.CostEstimate(flops=10**10, bytes_accessed=2**20, transcendentals=0),
        name="features",
    )(ids, activations, outs, in_proj, right)

    other = swapped(mine, 1)

    each = own * ex_count // tok_count
    own_scores = pl.pallas_call(
        own_scores_kernel,
        out_shape=jax.ShapeDtypeStruct((nb, own * len(masks)), jnp.float32),
        compiler_params=pltpu.CompilerParams(vmem_limit_bytes=8 * 1024 * 1024),
        cost_estimate=pl.CostEstimate(flops=10**10, bytes_accessed=2**20, transcendentals=0),
        name="own_scores",
    )(*pieces, mine)
    chunks = pl.pallas_call(
        lambda *refs: scores_kernel(ex_count, tok_count, own, masks, *refs),
        out_shape=jax.ShapeDtypeStruct((ex_count * tok_count, EX_DEV * each), jnp.float32),
        compiler_params=pltpu.CompilerParams(vmem_limit_bytes=8 * 1024 * 1024),
        name="scores",
    )(jnp.full((1, 2 * r), place), *pieces, own_scores, ids, other)
    arrived = lax.all_to_all(chunks, ("ex", "tok"), split_axis=0, concat_axis=0, tiled=True)
    total = jnp.sum(arrived, axis=0) * (1.0 / (r * size))
    return total.reshape(EX_DEV, each).T


def solution(mesh):
    placed = (
        P(("ex", "tok"), None, None),
        P(("ex", "tok"), None, None, None),
        P(("ex", "tok")),
        P(("ex", "tok"), None),
        P(("ex", "tok")),
        P(),
        P(),
        P("ex", None),
        P(),
    )
    return jax.shard_map(
        on_device, mesh=mesh, in_specs=placed, out_specs=P("tok", "ex"), check_vma=False
    )
```

```python
import functools

import jax
import jax.numpy as jnp
from jax import lax
from jax.experimental import pallas as pl
from jax.experimental.pallas import tpu as pltpu
from jax.sharding import PartitionSpec as P

EX_DEV = 4
SUB = 4
STEP = 8
WIDE = 16
HIGHEST = lax.Precision.HIGHEST
PLAIN = (((1,), (0,)), ((), ()))
NT = (((1,), (1,)), ((), ()))
TN = (((0,), (0,)), ((), ()))
VMEM = pl.BlockSpec(memory_space=pltpu.VMEM)


def split(x):
    high = x.astype(jnp.bfloat16)
    return high, (x - high.astype(jnp.float32)).astype(jnp.bfloat16)


def mm(a, b, dims=PLAIN):
    return lax.dot_general(a, b, dims, preferred_element_type=jnp.float32)


def exact(a, b, dims=PLAIN):
    return lax.dot_general(a, b, dims, precision=HIGHEST, preferred_element_type=jnp.float32)


def iota(shape, axis):
    return lax.broadcasted_iota(jnp.int32, shape, axis)


def diagonal(parts):
    zero = jnp.zeros_like(parts[0])
    return jnp.concatenate(
        [
            jnp.concatenate([x if k == l else zero for k in range(len(parts))], axis=1)
            for l, x in enumerate(parts)
        ],
        axis=0,
    )


def factors_kernel(precond_ref, left_ref, right_ref):
    layers, r = precond_ref.shape[0], precond_ref.shape[-1]
    row, col = iota((r, r), 0), iota((r, r), 1)
    order = (col == 2 * (row % (r // 2)) + row // (r // 2)).astype(jnp.float32)
    left = diagonal([exact(order, precond_ref[l, 0], NT) for l in range(layers)])
    left_ref[...] = jnp.concatenate(split(left), axis=0)
    for l in range(layers):
        high, low = split(diagonal([precond_ref[l, 1]] * 2))
        zero = jnp.zeros_like(high)
        right_ref[l] = jnp.concatenate(
            [jnp.concatenate([high, low], axis=1), jnp.concatenate([high, zero], axis=1)], axis=0
        )


def outputs_kernel(len_ref, grad_ref, w_ref, left_ref, out_ref, raw_ref):
    nb, size, layers, depth = grad_ref.shape
    width = left_ref.shape[1]
    rows = STEP * size
    lane_layer = iota((rows, width), 1) // (width // layers)
    slot = iota((size, width), 0)

    def turn(i, carry):
        grads = grad_ref[pl.ds(i * STEP, STEP)].reshape(rows * layers, depth)
        raw_ref[...] = mm(grads, w_ref[...], NT)
        out = raw_ref[pl.ds(0, rows, stride=layers), :]
        for l in range(1, layers):
            out = jnp.where(lane_layer == l, raw_ref[pl.ds(l, rows, stride=layers), :], out)
        lens = [len_ref[pl.ds(i * STEP + j, 1), :] for j in range(STEP)]
        live = jnp.concatenate([slot < x for x in lens], axis=0)
        high, low = split(jnp.where(live, out, 0.0))
        both = mm(left_ref[...], high, NT)
        done = both[:width] + both[width:] + mm(left_ref[:width], low, NT)
        here = pl.ds(pl.multiple_of(i * rows, rows), rows)
        out_ref[0, :, here], out_ref[1, :, here] = split(done)
        return carry

    lax.fori_loop(0, nb // STEP, turn, 0)


def features_kernel(id_ref, act_ref, out_ref, w_ref, feat_ref, in_ref):
    nb, size, depth = act_ref.shape
    width = out_ref.shape[1]
    r = feat_ref.shape[1] // 2
    layers, half = width // r, r // 2
    rows = SUB * size
    low_lane = iota((half, 2 * r), 1) < r
    lane_block = iota((r, rows), 1) // size

    def finish(i):
        proj_in = in_ref[i % 2]
        for s in range(WIDE // SUB):
            start = (i * WIDE + s * SUB) * size
            for l in range(layers):
                outs = [out_ref[k, l * r : (l + 1) * r, start : start + rows] for k in (0, 1)]
                x = proj_in[s * rows : (s + 1) * rows, l * r : (l + 1) * r]
                ih, il = split(jnp.concatenate([x, x], axis=1))
                lhs = jnp.concatenate(
                    [
                        jnp.concatenate(
                            [jnp.where(lane_block == j, o, jnp.zeros_like(o)) for o in outs], axis=1
                        )
                        for j in range(SUB)
                    ],
                    axis=0,
                )
                rhs = jnp.concatenate(
                    [
                        jnp.concatenate([ih, il], axis=1),
                        jnp.concatenate([ih, jnp.zeros_like(il)], axis=1),
                    ],
                    axis=0,
                )
                got = mm(lhs, rhs)
                got = got[:, : 2 * r] + got[:, 2 * r :]
                for j in range(SUB):
                    b = i * WIDE + s * SUB + j
                    here = (b * layers + l) * half
                    feat_ref[here : here + half] = jnp.where(
                        low_lane, got[j * r : j * r + half], got[j * r + half : (j + 1) * r]
                    )

    for i in range(nb // WIDE):
        acts = act_ref[pl.ds(i * WIDE, WIDE)].reshape(WIDE * size, depth)
        in_ref[i % 2] = mm(acts, w_ref[...])
        if i > 0:
            finish(i - 1)
    finish(nb // WIDE - 1)
    feat_ref[layers * half * nb :] = id_ref[...]


def products(q_ref, feat_ref):
    lanes = feat_ref.shape[1]
    groups = q_ref.shape[1] // lanes
    nb = feat_ref.shape[0] // groups
    count = q_ref.shape[0] // 2
    acc = jnp.zeros((2 * nb, 2 * count), jnp.float32)
    for g in range(0, groups, 2):
        f = [feat_ref[pl.ds(g + d, nb, stride=groups), :] for d in (0, 1)]
        f = jnp.concatenate(split(jnp.concatenate(f, axis=1)), axis=0)
        acc = acc + mm(f, q_ref[:, g * lanes : (g + 2) * lanes], NT)
    acc = acc[:nb] + acc[nb:]
    return acc[:, :count] + acc[:, count:]


def own_scores_kernel(*refs):
    *pieces, right_ref, mine_ref, score_ref, q_ref = refs
    layers, lanes = right_ref.shape[0], mine_ref.shape[1]
    groups = q_ref.shape[1] // lanes
    count, some = q_ref.shape[0] // 2, groups // layers // 4
    for begin in range(0, groups, some):
        here = [slice(g * lanes, (g + 1) * lanes) for g in range(begin, begin + some)]
        q = jnp.concatenate([ref[:, x] for x in here for ref in pieces], axis=0)
        q = mm(jnp.concatenate(split(q), axis=1), right_ref[begin * layers // groups])
        high, low = split(q[:, :lanes] + q[:, lanes:])
        for k, x in enumerate(here):
            rows = slice(k * count, (k + 1) * count)
            q_ref[:, x] = jnp.concatenate([high[rows], low[rows]], axis=0)
    score_ref[...] = products(q_ref, mine_ref)


def scores_kernel(ex_count, tok_count, own, masks, place_ref, q_ref, own_ref, id_ref, other_ref, out_ref):
    acc = jnp.concatenate([own_ref[...], products(q_ref, other_ref)], axis=0)
    blocks, count = acc.shape

    queries = own * ex_count
    piece = iota((count, queries), 0) // own
    mask = jnp.zeros((count, queries), jnp.int32)
    for k, m in enumerate(masks):
        mask = jnp.where(piece == k, m, mask)
    query = jnp.bitwise_xor(mask, place_ref[:, :1]) * own + iota((count, queries), 0) % own
    order = (query == iota((count, queries), 1)).astype(jnp.float32).astype(jnp.bfloat16)
    high, low = split(acc)
    acc = mm(high, order) + mm(low, order)
    targets = out_ref.shape[0]
    last = other_ref.shape[0] - id_ref.shape[0]
    ids = [ref[start : start + 1, : blocks // 2] for ref, start in ((id_ref, 0), (other_ref, last))]
    ids = jnp.concatenate(ids, axis=1).astype(jnp.int32)
    row = iota((targets * EX_DEV, blocks), 0)
    owner = row % targets // tok_count * EX_DEV + row // targets == ids
    owner = owner.astype(jnp.float32).astype(jnp.bfloat16)
    high, low = split(acc)
    full = mm(owner, high) + mm(owner, low)
    each = queries // tok_count
    tok = iota((targets * EX_DEV, each), 0) % tok_count
    result = full[:, :each]
    for t in range(1, tok_count):
        result = jnp.where(tok == t, full[:, t * each : (t + 1) * each], result)
    out_ref[...] = jnp.concatenate(
        [result[k * targets : (k + 1) * targets] for k in range(EX_DEV)], axis=1
    )


def on_device(
    activations,
    out_grads,
    block_len,
    block_dest,
    block_slot,
    in_proj,
    out_proj,
    query_grads,
    precond,
):
    nb, size, depth = activations.shape
    layers, grad_depth, r = out_proj.shape
    half = r // 2
    ex_count, tok_count = lax.axis_size("ex"), lax.axis_size("tok")
    own = query_grads.shape[0]
    place = lax.axis_index("ex").astype(jnp.int32)

    def swapped(x, mask):
        return lax.ppermute(x, "ex", [(i, i ^ mask) for i in range(ex_count)])

    width = layers * r
    left, right = pl.pallas_call(
        factors_kernel,
        out_shape=[
            jax.ShapeDtypeStruct((2 * width, width), jnp.bfloat16),
            jax.ShapeDtypeStruct((layers, 4 * r, 4 * r), jnp.bfloat16),
        ],
        compiler_params=pltpu.CompilerParams(vmem_limit_bytes=4 * 1024 * 1024),
        cost_estimate=pl.CostEstimate(flops=10**10, bytes_accessed=2**20, transcendentals=0),
        name="factors",
    )(precond)
    lens = jnp.broadcast_to(block_len[:, None], (nb, width))
    outs = pl.pallas_call(
        outputs_kernel,
        in_specs=[pl.BlockSpec(), VMEM, pl.BlockSpec(), pl.BlockSpec()],
        out_shape=jax.ShapeDtypeStruct((2, width, nb * size), jnp.bfloat16),
        scratch_shapes=[pltpu.VMEM((STEP * size * layers, width), jnp.float32)],
        compiler_params=pltpu.CompilerParams(vmem_limit_bytes=8 * 1024 * 1024),
        cost_estimate=pl.CostEstimate(flops=10**10, bytes_accessed=2**20, transcendentals=0),
        name="outputs",
    )(lens, out_grads, jnp.swapaxes(out_proj, 1, 2).reshape(width, grad_depth), left)

    held, masks = query_grads, [0]
    bit = ex_count // 2
    while bit > 4:
        held = jnp.concatenate([held, swapped(held, bit)], axis=0)
        masks = masks + [mask ^ bit for mask in masks]
        bit //= 2
    last = [bit] if bit == 2 else [6, 2, 4] if bit == 4 else []
    held, outs = lax.optimization_barrier((held, outs))
    pieces = [held] + [swapped(held, m) for m in last]
    masks = tuple(mask ^ m for m in [0] + last for mask in masks)

    ids = (block_dest[:, 0] * EX_DEV + block_slot).astype(jnp.float32)
    ids = jnp.broadcast_to(jnp.pad(ids, (0, 2 * r - nb))[None], (8, 2 * r))
    mine = pl.pallas_call(
        features_kernel,
        in_specs=[pl.BlockSpec(), VMEM, pl.BlockSpec(), VMEM],
        out_shape=jax.ShapeDtypeStruct((layers * half * nb + 8, 2 * r), jnp.float32),
        scratch_shapes=[pltpu.VMEM((2, WIDE * size, width), jnp.float32)],
        compiler_params=pltpu.CompilerParams(vmem_limit_bytes=12 * 1024 * 1024),
        cost_estimate=pl.CostEstimate(flops=10**10, bytes_accessed=2**20, transcendentals=0),
        name="features",
    )(ids, activations, outs, in_proj)

    other = swapped(mine, 1)

    each = own * ex_count // tok_count
    own_scores, split_queries = pl.pallas_call(
        own_scores_kernel,
        out_shape=[
            jax.ShapeDtypeStruct((nb, own * len(masks)), jnp.float32),
            jax.ShapeDtypeStruct((2 * own * len(masks), query_grads.shape[1]), jnp.bfloat16),
        ],
        compiler_params=pltpu.CompilerParams(vmem_limit_bytes=8 * 1024 * 1024),
        cost_estimate=pl.CostEstimate(flops=10**10, bytes_accessed=2**20, transcendentals=0),
        name="own_scores",
    )(*pieces, right, mine)
    chunks = pl.pallas_call(
        functools.partial(scores_kernel, ex_count, tok_count, own, masks),
        out_shape=jax.ShapeDtypeStruct((ex_count * tok_count, EX_DEV * each), jnp.float32),
        compiler_params=pltpu.CompilerParams(vmem_limit_bytes=8 * 1024 * 1024),
        name="scores",
    )(jnp.full((1, 2 * r), place), split_queries, own_scores, ids, other)
    arrived = lax.all_to_all(chunks, ("ex", "tok"), split_axis=0, concat_axis=0, tiled=True)
    total = jnp.sum(arrived, axis=0) * (1.0 / (r * size))
    return total.reshape(EX_DEV, each).T


def solution(mesh):
    placed = (
        P(("ex", "tok"), None, None),
        P(("ex", "tok"), None, None, None),
        P(("ex", "tok")),
        P(("ex", "tok"), None),
        P(("ex", "tok")),
        P(),
        P(),
        P("ex", None),
        P(),
    )
    return jax.shard_map(
        on_device, mesh=mesh, in_specs=placed, out_specs=P("tok", "ex"), check_vma=False
    )
```

```python
import functools

import jax
import jax.numpy as jnp
from jax import lax
from jax.experimental import pallas as pl
from jax.experimental.pallas import tpu as pltpu
from jax.sharding import PartitionSpec as P

EX_DEV = 4
SUB = 4
STEP = 8
WIDE = 8
HIGHEST = lax.Precision.HIGHEST
PLAIN = (((1,), (0,)), ((), ()))
NT = (((1,), (1,)), ((), ()))
TN = (((0,), (0,)), ((), ()))
VMEM = pl.BlockSpec(memory_space=pltpu.VMEM)


def split(x):
    high = x.astype(jnp.bfloat16)
    return high, (x - high.astype(jnp.float32)).astype(jnp.bfloat16)


def mm(a, b, dims=PLAIN):
    return lax.dot_general(a, b, dims, preferred_element_type=jnp.float32)


def exact(a, b, dims=PLAIN):
    return lax.dot_general(a, b, dims, precision=HIGHEST, preferred_element_type=jnp.float32)


def iota(shape, axis):
    return lax.broadcasted_iota(jnp.int32, shape, axis)


def diagonal(parts):
    zero = jnp.zeros_like(parts[0])
    return jnp.concatenate(
        [
            jnp.concatenate([x if k == l else zero for k in range(len(parts))], axis=1)
            for l, x in enumerate(parts)
        ],
        axis=0,
    )


def factors_kernel(precond_ref, left_ref, right_ref):
    layers, r = precond_ref.shape[0], precond_ref.shape[-1]
    row, col = iota((r, r), 0), iota((r, r), 1)
    order = (col == 2 * (row % (r // 2)) + row // (r // 2)).astype(jnp.float32)
    left = diagonal([exact(order, precond_ref[l, 0], NT) for l in range(layers)])
    left_ref[...] = jnp.concatenate(split(left), axis=0)
    for l in range(layers):
        high, low = split(diagonal([precond_ref[l, 1]] * 2))
        zero = jnp.zeros_like(high)
        right_ref[l] = jnp.concatenate(
            [jnp.concatenate([high, low], axis=1), jnp.concatenate([high, zero], axis=1)], axis=0
        )


def outputs_kernel(len_ref, grad_ref, w_ref, left_ref, out_ref, raw_ref):
    nb, size, layers, depth = grad_ref.shape
    width = left_ref.shape[1]
    rows = STEP * size
    lane_layer = iota((rows, width), 1) // (width // layers)
    slot = iota((size, width), 0)

    def turn(i, carry):
        grads = grad_ref[pl.ds(i * STEP, STEP)].reshape(rows * layers, depth)
        raw_ref[...] = mm(grads, w_ref[...], NT)
        out = raw_ref[pl.ds(0, rows, stride=layers), :]
        for l in range(1, layers):
            out = jnp.where(lane_layer == l, raw_ref[pl.ds(l, rows, stride=layers), :], out)
        lens = [len_ref[pl.ds(i * STEP + j, 1), :] for j in range(STEP)]
        live = jnp.concatenate([slot < x for x in lens], axis=0)
        high, low = split(jnp.where(live, out, 0.0))
        both = mm(left_ref[...], high, NT)
        done = both[:width] + both[width:] + mm(left_ref[:width], low, NT)
        here = pl.ds(pl.multiple_of(i * rows, rows), rows)
        out_ref[0, :, here], out_ref[1, :, here] = split(done)
        return carry

    lax.fori_loop(0, nb // STEP, turn, 0)


def features_kernel(id_ref, act_ref, out_ref, w_ref, feat_ref, in_ref):
    nb, size, depth = act_ref.shape
    width = out_ref.shape[1]
    r = feat_ref.shape[1] // 2
    layers, half = width // r, r // 2
    rows = SUB * size
    low_lane = iota((half, 2 * r), 1) < r
    lane_block = iota((r, rows), 1) // size

    def finish(i):
        proj_in = in_ref[i % 2]
        for s in range(WIDE // SUB):
            start = (i * WIDE + s * SUB) * size
            for l in range(layers):
                outs = [out_ref[k, l * r : (l + 1) * r, start : start + rows] for k in (0, 1)]
                x = proj_in[s * rows : (s + 1) * rows, l * r : (l + 1) * r]
                ih, il = split(jnp.concatenate([x, x], axis=1))
                lhs = jnp.concatenate(
                    [
                        jnp.concatenate(
                            [jnp.where(lane_block == j, o, jnp.zeros_like(o)) for o in outs], axis=1
                        )
                        for j in range(SUB)
                    ],
                    axis=0,
                )
                rhs = jnp.concatenate(
                    [
                        jnp.concatenate([ih, il], axis=1),
                        jnp.concatenate([ih, jnp.zeros_like(il)], axis=1),
                    ],
                    axis=0,
                )
                got = mm(lhs, rhs)
                got = got[:, : 2 * r] + got[:, 2 * r :]
                for j in range(SUB):
                    b = i * WIDE + s * SUB + j
                    here = (b * layers + l) * half
                    feat_ref[here : here + half] = jnp.where(
                        low_lane, got[j * r : j * r + half], got[j * r + half : (j + 1) * r]
                    )

    for i in range(nb // WIDE):
        acts = act_ref[pl.ds(i * WIDE, WIDE)].reshape(WIDE * size, depth)
        in_ref[i % 2] = mm(acts, w_ref[...])
        if i > 0:
            finish(i - 1)
    finish(nb // WIDE - 1)
    feat_ref[layers * half * nb :] = id_ref[...]


def products(q_ref, feat_ref):
    lanes = feat_ref.shape[1]
    groups = q_ref.shape[1] // lanes
    nb = feat_ref.shape[0] // groups
    count = q_ref.shape[0] // 2
    acc = jnp.zeros((2 * nb, 2 * count), jnp.float32)
    for g in range(0, groups, 2):
        f = [feat_ref[pl.ds(g + d, nb, stride=groups), :] for d in (0, 1)]
        f = jnp.concatenate(split(jnp.concatenate(f, axis=1)), axis=0)
        acc = acc + mm(f, q_ref[:, g * lanes : (g + 2) * lanes], NT)
    acc = acc[:nb] + acc[nb:]
    return acc[:, :count] + acc[:, count:]


def own_scores_kernel(*refs):
    *pieces, right_ref, mine_ref, score_ref, q_ref = refs
    layers, lanes = right_ref.shape[0], mine_ref.shape[1]
    groups = q_ref.shape[1] // lanes
    count, some = q_ref.shape[0] // 2, groups // layers // 2
    for begin in range(0, groups, some):
        here = [slice(g * lanes, (g + 1) * lanes) for g in range(begin, begin + some)]
        q = jnp.concatenate([ref[:, x] for x in here for ref in pieces], axis=0)
        q = mm(jnp.concatenate(split(q), axis=1), right_ref[begin * layers // groups])
        high, low = split(q[:, :lanes] + q[:, lanes:])
        for k, x in enumerate(here):
            rows = slice(k * count, (k + 1) * count)
            q_ref[:, x] = jnp.concatenate([high[rows], low[rows]], axis=0)
    score_ref[...] = products(q_ref, mine_ref)


def scores_kernel(ex_count, tok_count, own, masks, place_ref, q_ref, own_ref, id_ref, other_ref, out_ref):
    acc = jnp.concatenate([own_ref[...], products(q_ref, other_ref)], axis=0)
    blocks, count = acc.shape

    queries = own * ex_count
    piece = iota((count, queries), 0) // own
    mask = jnp.zeros((count, queries), jnp.int32)
    for k, m in enumerate(masks):
        mask = jnp.where(piece == k, m, mask)
    query = jnp.bitwise_xor(mask, place_ref[:, :1]) * own + iota((count, queries), 0) % own
    order = (query == iota((count, queries), 1)).astype(jnp.float32).astype(jnp.bfloat16)
    high, low = split(acc)
    acc = mm(high, order) + mm(low, order)
    targets = out_ref.shape[0]
    last = other_ref.shape[0] - id_ref.shape[0]
    ids = [ref[start : start + 1, : blocks // 2] for ref, start in ((id_ref, 0), (other_ref, last))]
    ids = jnp.concatenate(ids, axis=1).astype(jnp.int32)
    row = iota((targets * EX_DEV, blocks), 0)
    owner = row % targets // tok_count * EX_DEV + row // targets == ids
    owner = owner.astype(jnp.float32).astype(jnp.bfloat16)
    high, low = split(acc)
    full = mm(owner, high) + mm(owner, low)
    each = queries // tok_count
    tok = iota((targets * EX_DEV, each), 0) % tok_count
    result = full[:, :each]
    for t in range(1, tok_count):
        result = jnp.where(tok == t, full[:, t * each : (t + 1) * each], result)
    out_ref[...] = jnp.concatenate(
        [result[k * targets : (k + 1) * targets] for k in range(EX_DEV)], axis=1
    )


def on_device(
    activations,
    out_grads,
    block_len,
    block_dest,
    block_slot,
    in_proj,
    out_proj,
    query_grads,
    precond,
):
    nb, size, depth = activations.shape
    layers, grad_depth, r = out_proj.shape
    half = r // 2
    ex_count, tok_count = lax.axis_size("ex"), lax.axis_size("tok")
    own = query_grads.shape[0]
    place = lax.axis_index("ex").astype(jnp.int32)

    def swapped(x, mask):
        return lax.ppermute(x, "ex", [(i, i ^ mask) for i in range(ex_count)])

    width = layers * r
    left, right = pl.pallas_call(
        factors_kernel,
        out_shape=[
            jax.ShapeDtypeStruct((2 * width, width), jnp.bfloat16),
            jax.ShapeDtypeStruct((layers, 4 * r, 4 * r), jnp.bfloat16),
        ],
        compiler_params=pltpu.CompilerParams(vmem_limit_bytes=4 * 1024 * 1024),
        cost_estimate=pl.CostEstimate(flops=10**10, bytes_accessed=2**20, transcendentals=0),
        name="factors",
    )(precond)
    lens = jnp.broadcast_to(block_len[:, None], (nb, width))
    outs = pl.pallas_call(
        outputs_kernel,
        in_specs=[pl.BlockSpec(), VMEM, pl.BlockSpec(), pl.BlockSpec()],
        out_shape=jax.ShapeDtypeStruct((2, width, nb * size), jnp.bfloat16),
        scratch_shapes=[pltpu.VMEM((STEP * size * layers, width), jnp.float32)],
        compiler_params=pltpu.CompilerParams(vmem_limit_bytes=8 * 1024 * 1024),
        cost_estimate=pl.CostEstimate(flops=10**10, bytes_accessed=2**20, transcendentals=0),
        name="outputs",
    )(lens, out_grads, jnp.swapaxes(out_proj, 1, 2).reshape(width, grad_depth), left)

    held, masks = query_grads, [0]
    bit = ex_count // 2
    while bit > 4:
        held = jnp.concatenate([held, swapped(held, bit)], axis=0)
        masks = masks + [mask ^ bit for mask in masks]
        bit //= 2
    last = [bit] if bit == 2 else [6, 2, 4] if bit == 4 else []
    held, outs = lax.optimization_barrier((held, outs))
    pieces = [held] + [swapped(held, m) for m in last]
    masks = tuple(mask ^ m for m in [0] + last for mask in masks)

    ids = (block_dest[:, 0] * EX_DEV + block_slot).astype(jnp.float32)
    ids = jnp.broadcast_to(jnp.pad(ids, (0, 2 * r - nb))[None], (8, 2 * r))
    mine = pl.pallas_call(
        features_kernel,
        in_specs=[pl.BlockSpec(), VMEM, pl.BlockSpec(), VMEM],
        out_shape=jax.ShapeDtypeStruct((layers * half * nb + 8, 2 * r), jnp.float32),
        scratch_shapes=[pltpu.VMEM((2, WIDE * size, width), jnp.float32)],
        compiler_params=pltpu.CompilerParams(vmem_limit_bytes=12 * 1024 * 1024),
        cost_estimate=pl.CostEstimate(flops=10**10, bytes_accessed=2**20, transcendentals=0),
        name="features",
    )(ids, activations, outs, in_proj)

    other = swapped(mine, 1)

    each = own * ex_count // tok_count
    own_scores, split_queries = pl.pallas_call(
        own_scores_kernel,
        out_shape=[
            jax.ShapeDtypeStruct((nb, own * len(masks)), jnp.float32),
            jax.ShapeDtypeStruct((2 * own * len(masks), query_grads.shape[1]), jnp.bfloat16),
        ],
        compiler_params=pltpu.CompilerParams(vmem_limit_bytes=8 * 1024 * 1024),
        cost_estimate=pl.CostEstimate(flops=10**10, bytes_accessed=2**20, transcendentals=0),
        name="own_scores",
    )(*pieces, right, mine)
    chunks = pl.pallas_call(
        functools.partial(scores_kernel, ex_count, tok_count, own, masks),
        out_shape=jax.ShapeDtypeStruct((ex_count * tok_count, EX_DEV * each), jnp.float32),
        compiler_params=pltpu.CompilerParams(vmem_limit_bytes=8 * 1024 * 1024),
        name="scores",
    )(jnp.full((1, 2 * r), place), split_queries, own_scores, ids, other)
    arrived = lax.all_to_all(chunks, ("ex", "tok"), split_axis=0, concat_axis=0, tiled=True)
    total = jnp.sum(arrived, axis=0) * (1.0 / (r * size))
    return total.reshape(EX_DEV, each).T


def solution(mesh):
    placed = (
        P(("ex", "tok"), None, None),
        P(("ex", "tok"), None, None, None),
        P(("ex", "tok")),
        P(("ex", "tok"), None),
        P(("ex", "tok")),
        P(),
        P(),
        P("ex", None),
        P(),
    )
    return jax.shard_map(
        on_device, mesh=mesh, in_specs=placed, out_specs=P("tok", "ex"), check_vma=False
    )
```

```python
import functools

import jax
import jax.numpy as jnp
from jax import lax
from jax.experimental import pallas as pl
from jax.experimental.pallas import tpu as pltpu
from jax.sharding import PartitionSpec as P

EX_DEV = 4
SUB = 4
STEP = 8
WIDE = 8
HIGHEST = lax.Precision.HIGHEST
PLAIN = (((1,), (0,)), ((), ()))
NT = (((1,), (1,)), ((), ()))
TN = (((0,), (0,)), ((), ()))
VMEM = pl.BlockSpec(memory_space=pltpu.VMEM)


def split(x):
    high = x.astype(jnp.bfloat16)
    return high, (x - high.astype(jnp.float32)).astype(jnp.bfloat16)


def mm(a, b, dims=PLAIN):
    return lax.dot_general(a, b, dims, preferred_element_type=jnp.float32)


def exact(a, b, dims=PLAIN):
    return lax.dot_general(a, b, dims, precision=HIGHEST, preferred_element_type=jnp.float32)


def iota(shape, axis):
    return lax.broadcasted_iota(jnp.int32, shape, axis)


def diagonal(parts):
    zero = jnp.zeros_like(parts[0])
    return jnp.concatenate(
        [
            jnp.concatenate([x if k == l else zero for k in range(len(parts))], axis=1)
            for l, x in enumerate(parts)
        ],
        axis=0,
    )


def factors_kernel(precond_ref, left_ref, right_ref):
    layers, r = precond_ref.shape[0], precond_ref.shape[-1]
    row, col = iota((r, r), 0), iota((r, r), 1)
    order = (col == 2 * (row % (r // 2)) + row // (r // 2)).astype(jnp.float32)
    left = diagonal([exact(order, precond_ref[l, 0], NT) for l in range(layers)])
    left_ref[...] = jnp.concatenate(split(left), axis=0)
    for l in range(layers):
        high, low = split(diagonal([precond_ref[l, 1]] * 2))
        zero = jnp.zeros_like(high)
        right_ref[l] = jnp.concatenate(
            [jnp.concatenate([high, low], axis=1), jnp.concatenate([high, zero], axis=1)], axis=0
        )


def outputs_kernel(len_ref, grad_ref, w_ref, left_ref, out_ref, raw_ref):
    nb, size, layers, depth = grad_ref.shape
    width = left_ref.shape[1]
    rows = STEP * size
    lane_layer = iota((rows, width), 1) // (width // layers)
    slot = iota((size, width), 0)

    def turn(i, carry):
        grads = grad_ref[pl.ds(i * STEP, STEP)].reshape(rows * layers, depth)
        raw_ref[...] = mm(grads, w_ref[...], NT)
        out = raw_ref[pl.ds(0, rows, stride=layers), :]
        for l in range(1, layers):
            out = jnp.where(lane_layer == l, raw_ref[pl.ds(l, rows, stride=layers), :], out)
        lens = [len_ref[pl.ds(i * STEP + j, 1), :] for j in range(STEP)]
        live = jnp.concatenate([slot < x for x in lens], axis=0)
        high, low = split(jnp.where(live, out, 0.0))
        both = mm(left_ref[...], high, NT)
        done = both[:width] + both[width:] + mm(left_ref[:width], low, NT)
        here = pl.ds(pl.multiple_of(i * rows, rows), rows)
        out_ref[0, :, here], out_ref[1, :, here] = split(done)
        return carry

    lax.fori_loop(0, nb // STEP, turn, 0)


def features_kernel(id_ref, act_ref, out_ref, w_ref, feat_ref, in_ref):
    nb, size, depth = act_ref.shape
    width = out_ref.shape[1]
    r = feat_ref.shape[1] // 2
    layers, half = width // r, r // 2
    rows = SUB * size
    low_lane = iota((half, 2 * r), 1) < r
    lane_block = iota((r, rows), 1) // size

    def finish(i):
        proj_in = in_ref[i % 2]
        for s in range(WIDE // SUB):
            start = (i * WIDE + s * SUB) * size
            for l in range(layers):
                outs = [out_ref[k, l * r : (l + 1) * r, start : start + rows] for k in (0, 1)]
                x = proj_in[s * rows : (s + 1) * rows, l * r : (l + 1) * r]
                ih, il = split(jnp.concatenate([x, x], axis=1))
                lhs = jnp.concatenate(
                    [
                        jnp.concatenate(
                            [jnp.where(lane_block == j, o, jnp.zeros_like(o)) for o in outs], axis=1
                        )
                        for j in range(SUB)
                    ],
                    axis=0,
                )
                rhs = jnp.concatenate(
                    [
                        jnp.concatenate([ih, il], axis=1),
                        jnp.concatenate([ih, jnp.zeros_like(il)], axis=1),
                    ],
                    axis=0,
                )
                got = mm(lhs, rhs)
                got = got[:, : 2 * r] + got[:, 2 * r :]
                for j in range(SUB):
                    b = i * WIDE + s * SUB + j
                    here = (b * layers + l) * half
                    feat_ref[here : here + half] = jnp.where(
                        low_lane, got[j * r : j * r + half], got[j * r + half : (j + 1) * r]
                    )

    for i in range(nb // WIDE):
        acts = act_ref[pl.ds(i * WIDE, WIDE)].reshape(WIDE * size, depth)
        in_ref[i % 2] = mm(acts, w_ref[...])
        if i > 0:
            finish(i - 1)
    finish(nb // WIDE - 1)
    feat_ref[layers * half * nb :] = id_ref[...]


def pair(feat_ref, nb, groups, g):
    f = [feat_ref[pl.ds(g + d, nb, stride=groups), :] for d in (0, 1)]
    return jnp.concatenate(split(jnp.concatenate(f, axis=1)), axis=0)


def pairs_kernel(feat_ref, out_ref):
    nb = out_ref.shape[1] // 2
    groups = 2 * out_ref.shape[0]
    for g in range(0, groups, 2):
        out_ref[g // 2] = pair(feat_ref, nb, groups, g)


def products(q_ref, feat_ref):
    count = q_ref.shape[0] // 2
    if len(feat_ref.shape) == 3:
        nb, lanes = feat_ref.shape[1] // 2, feat_ref.shape[2] // 2
    else:
        lanes = feat_ref.shape[1]
        nb = feat_ref.shape[0] // (q_ref.shape[1] // lanes)
    groups = q_ref.shape[1] // lanes
    acc = jnp.zeros((2 * nb, 2 * count), jnp.float32)
    for g in range(0, groups, 2):
        f = feat_ref[g // 2] if len(feat_ref.shape) == 3 else pair(feat_ref, nb, groups, g)
        acc = acc + mm(f, q_ref[:, g * lanes : (g + 2) * lanes], NT)
    acc = acc[:nb] + acc[nb:]
    return acc[:, :count] + acc[:, count:]


def own_scores_kernel(*refs):
    *pieces, right_ref, mine_ref, score_ref, q_ref = refs
    layers, lanes = right_ref.shape[0], mine_ref.shape[2] // 2
    groups = q_ref.shape[1] // lanes
    count, some = q_ref.shape[0] // 2, groups // layers // 2
    for begin in range(0, groups, some):
        here = [slice(g * lanes, (g + 1) * lanes) for g in range(begin, begin + some)]
        q = jnp.concatenate([ref[:, x] for x in here for ref in pieces], axis=0)
        q = mm(jnp.concatenate(split(q), axis=1), right_ref[begin * layers // groups])
        high, low = split(q[:, :lanes] + q[:, lanes:])
        for k, x in enumerate(here):
            rows = slice(k * count, (k + 1) * count)
            q_ref[:, x] = jnp.concatenate([high[rows], low[rows]], axis=0)
    score_ref[...] = products(q_ref, mine_ref)


def scores_kernel(ex_count, tok_count, own, masks, place_ref, q_ref, own_ref, id_ref, other_ref, out_ref):
    acc = jnp.concatenate([own_ref[...], products(q_ref, other_ref)], axis=0)
    blocks, count = acc.shape

    queries = own * ex_count
    piece = iota((count, queries), 0) // own
    mask = jnp.zeros((count, queries), jnp.int32)
    for k, m in enumerate(masks):
        mask = jnp.where(piece == k, m, mask)
    query = jnp.bitwise_xor(mask, place_ref[:, :1]) * own + iota((count, queries), 0) % own
    order = (query == iota((count, queries), 1)).astype(jnp.float32).astype(jnp.bfloat16)
    high, low = split(acc)
    acc = mm(high, order) + mm(low, order)
    targets = out_ref.shape[0]
    last = other_ref.shape[0] - id_ref.shape[0]
    ids = [ref[start : start + 1, : blocks // 2] for ref, start in ((id_ref, 0), (other_ref, last))]
    ids = jnp.concatenate(ids, axis=1).astype(jnp.int32)
    row = iota((targets * EX_DEV, blocks), 0)
    owner = row % targets // tok_count * EX_DEV + row // targets == ids
    owner = owner.astype(jnp.float32).astype(jnp.bfloat16)
    high, low = split(acc)
    full = mm(owner, high) + mm(owner, low)
    each = queries // tok_count
    tok = iota((targets * EX_DEV, each), 0) % tok_count
    result = full[:, :each]
    for t in range(1, tok_count):
        result = jnp.where(tok == t, full[:, t * each : (t + 1) * each], result)
    out_ref[...] = jnp.concatenate(
        [result[k * targets : (k + 1) * targets] for k in range(EX_DEV)], axis=1
    )


def on_device(
    activations,
    out_grads,
    block_len,
    block_dest,
    block_slot,
    in_proj,
    out_proj,
    query_grads,
    precond,
):
    nb, size, depth = activations.shape
    layers, grad_depth, r = out_proj.shape
    half = r // 2
    ex_count, tok_count = lax.axis_size("ex"), lax.axis_size("tok")
    own = query_grads.shape[0]
    place = lax.axis_index("ex").astype(jnp.int32)

    def swapped(x, mask):
        return lax.ppermute(x, "ex", [(i, i ^ mask) for i in range(ex_count)])

    width = layers * r
    left, right = pl.pallas_call(
        factors_kernel,
        out_shape=[
            jax.ShapeDtypeStruct((2 * width, width), jnp.bfloat16),
            jax.ShapeDtypeStruct((layers, 4 * r, 4 * r), jnp.bfloat16),
        ],
        compiler_params=pltpu.CompilerParams(vmem_limit_bytes=4 * 1024 * 1024),
        cost_estimate=pl.CostEstimate(flops=10**10, bytes_accessed=2**20, transcendentals=0),
        name="factors",
    )(precond)
    lens = jnp.broadcast_to(block_len[:, None], (nb, width))
    outs = pl.pallas_call(
        outputs_kernel,
        in_specs=[pl.BlockSpec(), VMEM, pl.BlockSpec(), pl.BlockSpec()],
        out_shape=jax.ShapeDtypeStruct((2, width, nb * size), jnp.bfloat16),
        scratch_shapes=[pltpu.VMEM((STEP * size * layers, width), jnp.float32)],
        compiler_params=pltpu.CompilerParams(vmem_limit_bytes=8 * 1024 * 1024),
        cost_estimate=pl.CostEstimate(flops=10**10, bytes_accessed=2**20, transcendentals=0),
        name="outputs",
    )(lens, out_grads, jnp.swapaxes(out_proj, 1, 2).reshape(width, grad_depth), left)

    held, masks = query_grads, [0]
    bit = ex_count // 2
    while bit > 4:
        held = jnp.concatenate([held, swapped(held, bit)], axis=0)
        masks = masks + [mask ^ bit for mask in masks]
        bit //= 2
    last = [bit] if bit == 2 else [6, 2, 4] if bit == 4 else []
    held, outs = lax.optimization_barrier((held, outs))
    pieces = [held] + [swapped(held, m) for m in last]
    masks = tuple(mask ^ m for m in [0] + last for mask in masks)

    ids = (block_dest[:, 0] * EX_DEV + block_slot).astype(jnp.float32)
    ids = jnp.broadcast_to(jnp.pad(ids, (0, 2 * r - nb))[None], (8, 2 * r))
    mine = pl.pallas_call(
        features_kernel,
        in_specs=[pl.BlockSpec(), VMEM, pl.BlockSpec(), VMEM],
        out_shape=jax.ShapeDtypeStruct((layers * half * nb + 8, 2 * r), jnp.float32),
        scratch_shapes=[pltpu.VMEM((2, WIDE * size, width), jnp.float32)],
        compiler_params=pltpu.CompilerParams(vmem_limit_bytes=12 * 1024 * 1024),
        cost_estimate=pl.CostEstimate(flops=10**10, bytes_accessed=2**20, transcendentals=0),
        name="features",
    )(ids, activations, outs, in_proj)

    other = swapped(mine, 1)

    each = own * ex_count // tok_count
    pairs = pl.pallas_call(
        pairs_kernel,
        out_shape=jax.ShapeDtypeStruct((layers * half // 2, 2 * nb, 4 * r), jnp.bfloat16),
        compiler_params=pltpu.CompilerParams(vmem_limit_bytes=8 * 1024 * 1024),
        cost_estimate=pl.CostEstimate(flops=0, bytes_accessed=0, transcendentals=0),
        name="pairs",
    )(mine)
    own_scores, split_queries = pl.pallas_call(
        own_scores_kernel,
        out_shape=[
            jax.ShapeDtypeStruct((nb, own * len(masks)), jnp.float32),
            jax.ShapeDtypeStruct((2 * own * len(masks), query_grads.shape[1]), jnp.bfloat16),
        ],
        compiler_params=pltpu.CompilerParams(vmem_limit_bytes=8 * 1024 * 1024),
        cost_estimate=pl.CostEstimate(flops=10**10, bytes_accessed=2**20, transcendentals=0),
        name="own_scores",
    )(*pieces, right, pairs)
    chunks = pl.pallas_call(
        functools.partial(scores_kernel, ex_count, tok_count, own, masks),
        out_shape=jax.ShapeDtypeStruct((ex_count * tok_count, EX_DEV * each), jnp.float32),
        compiler_params=pltpu.CompilerParams(vmem_limit_bytes=8 * 1024 * 1024),
        name="scores",
    )(jnp.full((1, 2 * r), place), split_queries, own_scores, ids, other)
    arrived = lax.all_to_all(chunks, ("ex", "tok"), split_axis=0, concat_axis=0, tiled=True)
    total = jnp.sum(arrived, axis=0) * (1.0 / (r * size))
    return total.reshape(EX_DEV, each).T


def solution(mesh):
    placed = (
        P(("ex", "tok"), None, None),
        P(("ex", "tok"), None, None, None),
        P(("ex", "tok")),
        P(("ex", "tok"), None),
        P(("ex", "tok")),
        P(),
        P(),
        P("ex", None),
        P(),
    )
    return jax.shard_map(
        on_device, mesh=mesh, in_specs=placed, out_specs=P("tok", "ex"), check_vma=False
    )
```

```python
import functools

import jax
import jax.numpy as jnp
from jax import lax
from jax.experimental import pallas as pl
from jax.experimental.pallas import tpu as pltpu
from jax.sharding import PartitionSpec as P

EX_DEV = 4
SUB = 4
STEP = 8
WIDE = 8
HIGHEST = lax.Precision.HIGHEST
PLAIN = (((1,), (0,)), ((), ()))
NT = (((1,), (1,)), ((), ()))
TN = (((0,), (0,)), ((), ()))
VMEM = pl.BlockSpec(memory_space=pltpu.VMEM)


def split(x):
    high = x.astype(jnp.bfloat16)
    return high, (x - high.astype(jnp.float32)).astype(jnp.bfloat16)


def mm(a, b, dims=PLAIN):
    return lax.dot_general(a, b, dims, preferred_element_type=jnp.float32)


def exact(a, b, dims=PLAIN):
    return lax.dot_general(a, b, dims, precision=HIGHEST, preferred_element_type=jnp.float32)


def iota(shape, axis):
    return lax.broadcasted_iota(jnp.int32, shape, axis)


def diagonal(parts):
    zero = jnp.zeros_like(parts[0])
    return jnp.concatenate(
        [
            jnp.concatenate([x if k == l else zero for k in range(len(parts))], axis=1)
            for l, x in enumerate(parts)
        ],
        axis=0,
    )


def factors_kernel(precond_ref, left_ref, right_ref):
    layers, r = precond_ref.shape[0], precond_ref.shape[-1]
    row, col = iota((r, r), 0), iota((r, r), 1)
    order = (col == 2 * (row % (r // 2)) + row // (r // 2)).astype(jnp.float32)
    left = diagonal([exact(order, precond_ref[l, 0], NT) for l in range(layers)])
    left_ref[...] = jnp.concatenate(split(left), axis=0)
    for l in range(layers):
        high, low = split(diagonal([precond_ref[l, 1]] * 2))
        zero = jnp.zeros_like(high)
        right_ref[l] = jnp.concatenate(
            [jnp.concatenate([high, low], axis=1), jnp.concatenate([high, zero], axis=1)], axis=0
        )


def outputs_kernel(len_ref, grad_ref, w_ref, left_ref, out_ref, raw_ref):
    nb, size, layers, depth = grad_ref.shape
    width = left_ref.shape[1]
    rows = STEP * size
    lane_layer = iota((rows, width), 1) // (width // layers)
    slot = iota((size, width), 0)

    def turn(i, carry):
        grads = grad_ref[pl.ds(i * STEP, STEP)].reshape(rows * layers, depth)
        raw_ref[...] = mm(grads, w_ref[...], NT)
        out = raw_ref[pl.ds(0, rows, stride=layers), :]
        for l in range(1, layers):
            out = jnp.where(lane_layer == l, raw_ref[pl.ds(l, rows, stride=layers), :], out)
        lens = [len_ref[pl.ds(i * STEP + j, 1), :] for j in range(STEP)]
        live = jnp.concatenate([slot < x for x in lens], axis=0)
        high, low = split(jnp.where(live, out, 0.0))
        both = mm(left_ref[...], high, NT)
        done = both[:width] + both[width:] + mm(left_ref[:width], low, NT)
        here = pl.ds(pl.multiple_of(i * rows, rows), rows)
        out_ref[0, :, here], out_ref[1, :, here] = split(done)
        return carry

    lax.fori_loop(0, nb // STEP, turn, 0)


def features_kernel(id_ref, act_ref, out_ref, w_ref, feat_ref, in_ref):
    nb, size, depth = act_ref.shape
    width = out_ref.shape[1]
    r = feat_ref.shape[1] // 2
    layers, half = width // r, r // 2
    rows = SUB * size
    low_lane = iota((half, 2 * r), 1) < r
    lane_block = iota((r, rows), 1) // size

    def finish(i):
        proj_in = in_ref[i % 2]
        for s in range(WIDE // SUB):
            start = (i * WIDE + s * SUB) * size
            for l in range(layers):
                outs = [out_ref[k, l * r : (l + 1) * r, start : start + rows] for k in (0, 1)]
                x = proj_in[s * rows : (s + 1) * rows, l * r : (l + 1) * r]
                ih, il = split(jnp.concatenate([x, x], axis=1))
                lhs = jnp.concatenate(
                    [
                        jnp.concatenate(
                            [jnp.where(lane_block == j, o, jnp.zeros_like(o)) for o in outs], axis=1
                        )
                        for j in range(SUB)
                    ],
                    axis=0,
                )
                rhs = jnp.concatenate(
                    [
                        jnp.concatenate([ih, il], axis=1),
                        jnp.concatenate([ih, jnp.zeros_like(il)], axis=1),
                    ],
                    axis=0,
                )
                got = mm(lhs, rhs)
                got = got[:, : 2 * r] + got[:, 2 * r :]
                for j in range(SUB):
                    b = i * WIDE + s * SUB + j
                    here = (b * layers + l) * half
                    feat_ref[here : here + half] = jnp.where(
                        low_lane, got[j * r : j * r + half], got[j * r + half : (j + 1) * r]
                    )

    for i in range(nb // WIDE):
        acts = act_ref[pl.ds(i * WIDE, WIDE)].reshape(WIDE * size, depth)
        in_ref[i % 2] = mm(acts, w_ref[...])
        if i > 0:
            finish(i - 1)
    finish(nb // WIDE - 1)
    feat_ref[layers * half * nb :] = id_ref[...]


def products(q_ref, feat_ref):
    lanes = feat_ref.shape[1]
    groups = q_ref.shape[1] // lanes
    nb = feat_ref.shape[0] // groups
    count = q_ref.shape[0] // 2
    acc = jnp.zeros((2 * nb, 2 * count), jnp.float32)
    for g in range(0, groups, 2):
        f = [feat_ref[pl.ds(g + d, nb, stride=groups), :] for d in (0, 1)]
        f = jnp.concatenate(split(jnp.concatenate(f, axis=1)), axis=0)
        acc = acc + mm(f, q_ref[:, g * lanes : (g + 2) * lanes], NT)
    acc = acc[:nb] + acc[nb:]
    return acc[:, :count] + acc[:, count:]


def own_scores_kernel(*refs):
    *pieces, right_ref, mine_ref, score_ref, q_ref = refs
    layers, lanes = right_ref.shape[0], mine_ref.shape[1]
    groups = q_ref.shape[1] // lanes
    count, some = q_ref.shape[0] // 2, groups // layers // 2
    for begin in range(0, groups, some):
        here = [slice(g * lanes, (g + 1) * lanes) for g in range(begin, begin + some)]
        q = jnp.concatenate([ref[:, x] for x in here for ref in pieces], axis=0)
        q = mm(jnp.concatenate(split(q), axis=1), right_ref[begin * layers // groups])
        high, low = split(q[:, :lanes] + q[:, lanes:])
        for k, x in enumerate(here):
            rows = slice(k * count, (k + 1) * count)
            q_ref[:, x] = jnp.concatenate([high[rows], low[rows]], axis=0)
    score_ref[...] = products(q_ref, mine_ref)


def scores_kernel(order_ref, target_ref, tok_ref, q_ref, own_ref, id_ref, other_ref, out_ref):
    acc = jnp.concatenate([own_ref[...], products(q_ref, other_ref)], axis=0)
    blocks = acc.shape[0]
    order = order_ref[...]
    queries = order.shape[1]
    high, low = split(acc)
    acc = mm(high, order) + mm(low, order)
    targets = out_ref.shape[0]
    last = other_ref.shape[0] - id_ref.shape[0]
    ids = [ref[start : start + 1, : blocks // 2] for ref, start in ((id_ref, 0), (other_ref, last))]
    owner = target_ref[...] == jnp.concatenate(ids, axis=1)
    owner = owner.astype(jnp.float32).astype(jnp.bfloat16)
    high, low = split(acc)
    full = mm(owner, high) + mm(owner, low)
    each = tok_ref.shape[1]
    result = full[:, :each]
    for t in range(1, queries // each):
        result = jnp.where(tok_ref[...] == t, full[:, t * each : (t + 1) * each], result)
    out_ref[...] = jnp.concatenate(
        [result[k * targets : (k + 1) * targets] for k in range(EX_DEV)], axis=1
    )


def on_device(
    activations,
    out_grads,
    block_len,
    block_dest,
    block_slot,
    in_proj,
    out_proj,
    query_grads,
    precond,
):
    nb, size, depth = activations.shape
    layers, grad_depth, r = out_proj.shape
    half = r // 2
    ex_count, tok_count = lax.axis_size("ex"), lax.axis_size("tok")
    own = query_grads.shape[0]
    place = lax.axis_index("ex").astype(jnp.int32)

    def swapped(x, mask):
        return lax.ppermute(x, "ex", [(i, i ^ mask) for i in range(ex_count)])

    width = layers * r
    left, right = pl.pallas_call(
        factors_kernel,
        out_shape=[
            jax.ShapeDtypeStruct((2 * width, width), jnp.bfloat16),
            jax.ShapeDtypeStruct((layers, 4 * r, 4 * r), jnp.bfloat16),
        ],
        compiler_params=pltpu.CompilerParams(vmem_limit_bytes=4 * 1024 * 1024),
        cost_estimate=pl.CostEstimate(flops=10**10, bytes_accessed=2**20, transcendentals=0),
        name="factors",
    )(precond)
    lens = jnp.broadcast_to(block_len[:, None], (nb, width))
    outs = pl.pallas_call(
        outputs_kernel,
        in_specs=[pl.BlockSpec(), VMEM, pl.BlockSpec(), pl.BlockSpec()],
        out_shape=jax.ShapeDtypeStruct((2, width, nb * size), jnp.bfloat16),
        scratch_shapes=[pltpu.VMEM((STEP * size * layers, width), jnp.float32)],
        compiler_params=pltpu.CompilerParams(vmem_limit_bytes=8 * 1024 * 1024),
        cost_estimate=pl.CostEstimate(flops=10**10, bytes_accessed=2**20, transcendentals=0),
        name="outputs",
    )(lens, out_grads, jnp.swapaxes(out_proj, 1, 2).reshape(width, grad_depth), left)

    held, masks = query_grads, [0]
    bit = ex_count // 2
    while bit > 4:
        held = jnp.concatenate([held, swapped(held, bit)], axis=0)
        masks = masks + [mask ^ bit for mask in masks]
        bit //= 2
    last = [bit] if bit == 2 else [6, 2, 4] if bit == 4 else []
    held, outs = lax.optimization_barrier((held, outs))
    pieces = [held] + [swapped(held, m) for m in last]
    masks = tuple(mask ^ m for m in [0] + last for mask in masks)

    ids = (block_dest[:, 0] * EX_DEV + block_slot).astype(jnp.float32)
    ids = jnp.broadcast_to(jnp.pad(ids, (0, 2 * r - nb))[None], (8, 2 * r))
    mine = pl.pallas_call(
        features_kernel,
        in_specs=[pl.BlockSpec(), VMEM, pl.BlockSpec(), VMEM],
        out_shape=jax.ShapeDtypeStruct((layers * half * nb + 8, 2 * r), jnp.float32),
        scratch_shapes=[pltpu.VMEM((2, WIDE * size, width), jnp.float32)],
        compiler_params=pltpu.CompilerParams(vmem_limit_bytes=12 * 1024 * 1024),
        cost_estimate=pl.CostEstimate(flops=10**10, bytes_accessed=2**20, transcendentals=0),
        name="features",
    )(ids, activations, outs, in_proj)

    other = swapped(mine, 1)

    each = own * ex_count // tok_count
    own_scores, split_queries = pl.pallas_call(
        own_scores_kernel,
        out_shape=[
            jax.ShapeDtypeStruct((nb, own * len(masks)), jnp.float32),
            jax.ShapeDtypeStruct((2 * own * len(masks), query_grads.shape[1]), jnp.bfloat16),
        ],
        compiler_params=pltpu.CompilerParams(vmem_limit_bytes=8 * 1024 * 1024),
        cost_estimate=pl.CostEstimate(flops=10**10, bytes_accessed=2**20, transcendentals=0),
        name="own_scores",
    )(*pieces, right, mine)
    query = (place ^ jnp.repeat(jnp.asarray(masks, jnp.int32), own)) * own
    query = query + jnp.arange(own * len(masks), dtype=jnp.int32) % own
    order = (query[:, None] == jnp.arange(own * ex_count)[None, :]).astype(jnp.bfloat16)
    targets = ex_count * tok_count
    row = jnp.arange(targets * EX_DEV, dtype=jnp.int32)[:, None]
    target = (row % targets // tok_count * EX_DEV + row // targets).astype(jnp.float32)
    target = jnp.broadcast_to(target, (targets * EX_DEV, 2 * nb))
    tok = jnp.broadcast_to((row % tok_count).astype(jnp.float32), (targets * EX_DEV, each))
    chunks = pl.pallas_call(
        scores_kernel,
        out_shape=jax.ShapeDtypeStruct((ex_count * tok_count, EX_DEV * each), jnp.float32),
        compiler_params=pltpu.CompilerParams(vmem_limit_bytes=8 * 1024 * 1024),
        name="scores",
    )(order, target, tok, split_queries, own_scores, ids, other)
    arrived = lax.all_to_all(chunks, ("ex", "tok"), split_axis=0, concat_axis=0, tiled=True)
    total = jnp.sum(arrived, axis=0) * (1.0 / (r * size))
    return total.reshape(EX_DEV, each).T


def solution(mesh):
    placed = (
        P(("ex", "tok"), None, None),
        P(("ex", "tok"), None, None, None),
        P(("ex", "tok")),
        P(("ex", "tok"), None),
        P(("ex", "tok")),
        P(),
        P(),
        P("ex", None),
        P(),
    )
    return jax.shard_map(
        on_device, mesh=mesh, in_specs=placed, out_specs=P("tok", "ex"), check_vma=False
    )
```
